256 devices in a mesh: dp: 32 (over z, y), expert: 8 (over x, core).
Axes of the slice: x: 4, y: 4, z: 8, core: 2. Of those that a mesh axis runs over, the one named last changes fastest.
Arguments:
- residual: bfloat16 [32768, 4096], P(('dp', 'expert')), may hold values from -36 to 36
- norm_gain: float32 [4096], replicated, may hold values from 0.5 to 1.5
- router_weight: bfloat16 [16, 4096], replicated, may hold values from -8 to 8
- up_weight: bfloat16 [4096, 16, 768], P('dp', 'expert'), may hold values from -0.09375 to 0.09375
- routes: int32 [32768, 2], P(('dp', 'expert')), may hold values from 0 to 15, all different within a row; in each aligned block of 128 rows (0 to 127, 128 to 255, ...) at most 20 rows name the same one
- keep_flags: int32 [32768, 2], P(('dp', 'expert')), may hold values 0 or 1
- gate_grad: float32 [32768, 2], P(('dp', 'expert')), may hold values from -24 to 24
- grad_hidden: bfloat16 [16, 5120, 768], P('expert', 'dp'), may hold values from -6 to 6
Outputs:
- resid_grad: bfloat16 [32768, 4096], P(('dp', 'expert'))
- up_grad: float32 [4096, 16, 768], P('dp', 'expert')
- router_grad: float32 [16, 4096], replicated
- gain_grad: float32 [4096], replicated
The draws below stay inside these ranges and needn't reach their ends.
Inputs may be any that keep to these rules, and one draw needn't show every extreme that they name: `routes`: within the 128 tokens of one device (aligned blocks of rows) no expert is named by more than 20 choices, and in every draw some expert is named by exactly 20; a token's two experts differ.
All inputs are finite; a program needn't handle non-finite values. No bound on the sum of `keep_flags` on one device may be relied on, other than what follows from the above.
Results may differ from the reference program's by a relative error of at most 0.02.
The reference program's roundings to bfloat16 on the way (of `normed`, `slot_rows`, `pre_grad`, `back_rows` and `logit_grad`) count: a program that leaves them out, or rounds other values in their place, can miss the bound.
Values may be sent and summed in bfloat16 or wider, within the bound.
A program may use at most 128 MiB of HBM per device.

```python
import math
import jax
import jax.numpy as jnp
import numpy as np
from jax import lax

D = 4096
FF = 768
TOPK = 2
TOK_DEV = 128
E = 16
CAP = 20
TOKENS = 32768
N_DP = 32


def draw_residual(key, part):
    key = jax.random.fold_in(key, 11)
    first, second, third = jax.random.split(key, 3)
    row_scale = jnp.exp(jax.random.uniform(first, (TOKENS, 1), jnp.float32, math.log(0.3), math.log(3.0)))
    col_scale = jnp.exp(jax.random.uniform(second, (1, D), jnp.float32, math.log(0.3), math.log(3.0)))
    base = jnp.clip(jax.random.normal(third, (TOKENS, D), jnp.float32), -4.0, 4.0)
    return (base * row_scale * col_scale).astype(jnp.bfloat16)


def draw_router_weight(key, part):
    key = jax.random.fold_in(key, 23)
    first = jax.random.fold_in(key, 0)
    noise = jnp.clip(jax.random.normal(first, (E, D), jnp.float32), -4.0, 4.0) * (2.0 / math.sqrt(D))
    return noise.astype(jnp.bfloat16)


def set_ends(array, key, smallest, top_value):
    dims = array.shape
    spot = [jax.random.randint(jax.random.fold_in(key, axis), (), 0, dims[axis]) for axis in range(len(dims))]
    array = array.at[tuple(spot)].set(smallest)
    longest = dims.index(max(dims))
    spot[longest] = (spot[longest] + 1) % dims[longest]
    return array.at[tuple(spot)].set(top_value)


def steps_of(key, dims, pieces, smallest, high):
    factor_of, own = 1.0, jax.random.fold_in(key, 6)
    for dim, shards_of in pieces:
        heights = jnp.exp(jax.random.uniform(jax.random.fold_in(own, dim), (shards_of,), jnp.float32, smallest / len(pieces), high / len(pieces)))
        factor_of = factor_of * jnp.repeat(heights, dims[dim] // shards_of).reshape([-1 if axis == dim else 1 for axis in range(len(dims))])
    return factor_of


def shared_out(key, own, number, rows, count, top, most, lean):
    order = jax.random.permutation(key, count)
    packed, usual = load_shares(count, rows * top, most, lean, True), load_shares(count, rows * top, most, lean, False)
    places = jnp.arange(count)

    def named(lengths, turn):
        used = int((lengths > 0).sum())
        fixed = max(1, used // 4)
        passed = fixed + (places - fixed + turn * (used - fixed)) % max(1, count - fixed)
        return jnp.zeros((count,), jnp.int32).at[order[jnp.where(places < fixed, places, passed)]].set(jnp.asarray(lengths, jnp.int32))

    lengths = jnp.where(number % 4 == 0, named(packed, number // 4), named(usual, number - number // 4 - 1))
    mixed = jax.random.permutation(jax.random.fold_in(own, 3), count)
    donor, receiver = mixed[0:count // 2 * 2:2], mixed[1:count // 2 * 2:2]
    slack = jnp.minimum(lengths[donor] - 1, most - lengths[receiver]) // 2
    slack = jnp.where((donor == order[0]) | (receiver == order[0]) | (lengths[receiver] == 0), 0, jnp.maximum(slack, 0))
    passed = jax.random.randint(jax.random.fold_in(own, 4), (count // 2,), 0, 1 << 20) % (slack + 1)
    lengths = lengths.at[donor].add(-passed).at[receiver].add(passed)
    members = jnp.searchsorted(jnp.cumsum(lengths), jnp.arange(rows * top), side="right").astype(jnp.int32)
    grid = members.reshape(top, rows).T
    grid = grid[jax.random.permutation(jax.random.fold_in(own, 1), rows)]
    turn = jax.random.randint(jax.random.fold_in(own, 2), (rows, 1), 0, top)
    return jnp.take_along_axis(grid, (jnp.arange(top)[None, :] + turn) % top, axis=1)


def load_shares(number_of, total, reach, slope, full):
    loads = [(1 << 20) // math.isqrt(rank ** slope) + 1 for rank in range(1, number_of + 1)]
    largest = reach if full else min(reach, max(-(-total // number_of), total * loads[0] // sum(loads)))
    least = 1 if total - largest >= number_of - 1 else 0
    holding, spare = [largest] + [least] * (number_of - 1), total - largest - least * (number_of - 1)
    while spare > 0:
        free = [i for i in range(1, number_of) if holding[i] < largest] or [i for i in range(1, number_of) if holding[i] < reach]
        mass, left = sum([loads[i] for i in free]), spare
        for i in free:
            addition = min(reach - holding[i], max(1, left * loads[i] // mass), spare)
            holding[i] = holding[i] + addition
            spare = spare - addition
    return np.array(holding)


def centred(rng, shape, width, bound, pieces=(), held_as=jnp.bfloat16):
    loudness = steps_of(rng, shape, pieces, -0.22, 0.18) if pieces else 1.0
    array = jax.random.normal(rng, shape, jnp.float32) * width * loudness
    return jnp.minimum(jnp.maximum(array, -bound), bound).astype(held_as)


def setup_inputs(seed: int = 0) -> dict:
    arg_keys = jax.random.split(jax.random.key(seed), 9)
    residual = draw_residual(jax.random.fold_in(arg_keys[8], 71), 0)
    norm_gain = jnp.clip(1.0 + 0.1 * jax.random.normal(arg_keys[1], (D,), jnp.float32), 0.5, 1.5)
    router_weight = draw_router_weight(jax.random.fold_in(arg_keys[8], 71), 0)
    up_weight = centred(arg_keys[3], (D, E, FF), D ** -0.5, 0.09375, ((0, 32), (1, 8)))
    routes_keys = jax.random.split(jax.random.fold_in(arg_keys[4], 1), TOKENS // TOK_DEV)
    routes_turns = jax.random.permutation(jax.random.fold_in(arg_keys[4], 3), TOKENS // TOK_DEV)
    routes = jax.vmap(lambda own, number: shared_out(jax.random.fold_in(arg_keys[4], 2), own, number, TOK_DEV, E, TOPK, CAP, 2))(routes_keys, routes_turns).reshape((TOKENS, TOPK))
    keep_flags = set_ends((jax.random.randint(arg_keys[5], (TOKENS, TOPK), 0, 8) < 7).astype(jnp.int32), jax.random.fold_in(arg_keys[5], 1), 0, 1)
    gate_grad = centred(arg_keys[6], (TOKENS, TOPK), 4.0, 24.0, ((0, 256),), jnp.float32)
    grad_hidden = centred(arg_keys[7], (E, TOKENS // TOK_DEV * CAP, FF), 1.0, 6.0, ((0, 8), (1, 32)))
    return dict(residual=residual, norm_gain=norm_gain, router_weight=router_weight, up_weight=up_weight, routes=routes, keep_flags=keep_flags, gate_grad=gate_grad, grad_hidden=grad_hidden)


def silu_slope(preact):
    sigmoid_value = jax.nn.sigmoid(preact)
    return sigmoid_value * (1.0 + preact * (1.0 - sigmoid_value))

def slot_table(routes):
    blocks = routes.reshape(TOKENS // TOK_DEV, TOK_DEV * TOPK)
    member = (blocks[:, :, None] == jnp.arange(E, dtype=jnp.int32)[None, None, :]).astype(jnp.int32)
    ahead = jnp.cumsum(member, axis=1) - member
    return lax.optimization_barrier(jnp.sum(ahead * member, axis=2)).reshape(TOKENS, TOPK).astype(jnp.int32)

def reference(residual, norm_gain, router_weight, up_weight, routes, keep_flags, gate_grad, grad_hidden):
    wide_rows = residual.astype(jnp.float32)
    inv_rms = lax.rsqrt(lax.optimization_barrier(jnp.mean(wide_rows * wide_rows, axis=1, keepdims=True)) + 1e-06)
    normed = (wide_rows * inv_rms * norm_gain[None, :]).astype(jnp.bfloat16)
    slot = slot_table(routes)
    device_of = (jnp.arange(TOKENS, dtype=jnp.int32) // TOK_DEV)[:, None]
    position = (device_of * CAP + slot).astype(jnp.int32)
    slot_count = TOKENS // TOK_DEV * CAP
    token_ids = jnp.broadcast_to(jnp.arange(TOKENS, dtype=jnp.int32)[:, None], (TOKENS, TOPK))
    padded = jnp.concatenate([normed, jnp.zeros((1, D), normed.dtype)], axis=0)

    def one_expert(expert):
        chosen = (routes == expert) & (keep_flags == 1)
        target = jnp.where(chosen, position, slot_count).astype(jnp.int32)
        table = jnp.full((slot_count,), TOKENS, jnp.int32)
        table = table.at[target.reshape(-1)].set(token_ids.reshape(-1), mode='drop')
        slot_rows = padded[table]
        weight = up_weight[:, expert, :]
        preact = jnp.dot(slot_rows, weight, preferred_element_type=jnp.float32)
        pre_grad = (grad_hidden[expert].astype(jnp.float32) * silu_slope(preact)).astype(jnp.bfloat16)
        back_rows = jnp.dot(pre_grad, weight.T, preferred_element_type=jnp.float32).astype(jnp.bfloat16)
        grouped_rows = slot_rows.reshape(N_DP, slot_count // N_DP, D)
        grouped_grad = pre_grad.reshape(N_DP, slot_count // N_DP, FF)

        def add_group(total, pair):
            partial_sum = jnp.dot(pair[0].T, pair[1], preferred_element_type=jnp.float32)
            rounded = lax.optimization_barrier(partial_sum.astype(jnp.bfloat16))
            return (total + rounded.astype(jnp.float32), None)
        weight_grad, _ = lax.scan(add_group, jnp.zeros((D, FF), jnp.float32), (grouped_rows, grouped_grad))
        return (back_rows, weight_grad)
    backs, grads = lax.map(one_expert, jnp.arange(E, dtype=jnp.int32))
    flat_back = backs.reshape(E * slot_count, D)
    from_experts = jnp.zeros((TOKENS, D), jnp.float32)
    for column in range(TOPK):
        lookup = (routes[:, column] * slot_count + position[:, column]).astype(jnp.int32)
        picked = flat_back[lookup].astype(jnp.float32)
        from_experts = from_experts + picked * keep_flags[:, column:column + 1].astype(jnp.float32)
    logits = jnp.dot(normed, router_weight.T, preferred_element_type=jnp.float32)
    probs = jax.nn.softmax(logits, axis=1)
    choose = (routes[:, :, None] == jnp.arange(E, dtype=jnp.int32)[None, None, :]).astype(jnp.float32)
    weighted = keep_flags.astype(jnp.float32) * gate_grad
    prob_grad = lax.optimization_barrier(jnp.sum(choose * weighted[:, :, None], axis=1))
    logit_grad = (probs * (prob_grad - lax.optimization_barrier(jnp.sum(probs * prob_grad, axis=1, keepdims=True)))).astype(jnp.bfloat16)
    router_grad = jnp.dot(logit_grad.T, normed, preferred_element_type=jnp.float32)
    total_grad = from_experts + jnp.dot(logit_grad, router_weight, preferred_element_type=jnp.float32)
    gain_grad = lax.optimization_barrier(jnp.sum(total_grad * wide_rows * inv_rms, axis=0))
    scaled = total_grad * norm_gain[None, :]
    inner = lax.optimization_barrier(jnp.mean(scaled * wide_rows, axis=1, keepdims=True))
    resid_grad = (inv_rms * scaled - wide_rows * inv_rms * inv_rms * inv_rms * inner).astype(jnp.bfloat16)
    return (resid_grad, grads.transpose(1, 0, 2), router_grad, gain_grad)
```

```python
import functools

import jax
import jax.numpy as jnp
import numpy as np
from jax import lax
from jax.experimental import pallas as pl
from jax.experimental.pallas import tpu as pltpu
from jax.sharding import PartitionSpec as P

NY = 4
BF16 = jnp.bfloat16
F32 = jnp.float32


def nn(a, b):
    return lax.dot_general(a, b, (((1,), (0,)), ((), ())), preferred_element_type=F32)


def nt(a, b):
    return lax.dot_general(a, b, (((1,), (1,)), ((), ())), preferred_element_type=F32)


def tn(a, b):
    return lax.dot_general(a, b, (((0,), (0,)), ((), ())), preferred_element_type=F32)


def silu_slope(v):
    s = jax.nn.sigmoid(v)
    return s * (1.0 + v * (1.0 - s))


class Dims:
    def __init__(self, mesh, tokens, width, ff, cap):
        self.nz = mesh.shape["dp"] // NY
        self.nx = mesh.shape["expert"]
        self.t = tokens
        self.d = width
        self.cb = width // (self.nz * NY)
        self.q = width // NY
        self.ff = ff
        self.cap = cap
        self.e = 2 * self.nx
        self.rows = NY * cap
        self.m = self.nx * self.rows
        self.blk = self.nx * cap


def kernel(
    c,
    residual,
    norm_gain,
    router_weight,
    weight,
    routes,
    keep,
    gate,
    grad_hidden,
    order,
    order_t,
    resid_out,
    up_out,
    router_out,
    gain_out,
    inv_ref,
    tok_send,
    tok,
    info,
    rw_slices,
    place,
    slots_out,
    slots,
    wfull,
    part,
    part_perm,
    rs_a,
    rs_b,
    pre_grad,
    pg_rows,
    backs,
    returned,
    wg_out,
    wg_in,
    acc,
    tok_back,
    tok_ret,
    gain_acc,
    ar0,
    ar1,
    ar2,
    ar3,
    ar4,
    sem_tok,
    sem_info,
    sem_slot,
    sem_w,
    sem_rs,
    sem_pg,
    sem_back,
    sem_wg,
    sem_ret,
    sem_ar,
):
    nz, nx, t, q, cb, cap, rows, m, blk = c.nz, c.nx, c.t, c.q, c.cb, c.cap, c.rows, c.m, c.blk
    half = nz // 2
    hb = blk // 2
    hc = cb // 2
    dp = lax.axis_index("dp")
    me = lax.axis_index("expert")
    z, y = dp // NY, dp % NY

    def at_y(d):
        return (y + d) % NY

    def at_z(d):
        return (z + d + nz) % nz

    def at_x(d):
        return (me + d) % nx

    def to_y(d):
        return {"dp": z * NY + at_y(d)}

    def to_z(d):
        return {"dp": at_z(d) * NY + y}

    def to_x(d):
        return {"expert": at_x(d)}

    def remote(src, dst, sems, index, target):
        return pltpu.make_async_remote_copy(
            src_ref=src,
            dst_ref=dst,
            send_sem=sems.at[(0, *index)],
            recv_sem=sems.at[(1, *index)],
            device_id=target,
            device_id_type=pl.DeviceIdType.MESH,
        )

    barrier = pltpu.get_barrier_semaphore()
    for d in range(1, NY):
        pl.semaphore_signal(barrier, inc=1, device_id=to_y(d))
    for d in range(1, nz):
        pl.semaphore_signal(barrier, inc=1, device_id=to_z(d))
    for d in range(1, nx):
        pl.semaphore_signal(barrier, inc=1, device_id=to_x(d))
    pl.semaphore_wait(barrier, NY + nz + nx - 3)

    for i in range(2):
        wfull[i, z] = weight[i]

    def w_copy(i, way, s):
        sign = 1 if way == 0 else -1
        source = at_z(-sign * (s - 1))
        ref = wfull.at[i, source]
        if s == half:
            ref = ref.at[pl.ds(way * hc, hc)]
        return remote(ref, ref, sem_w, (i, way, s - 1), to_z(sign))

    def w_recv(i, way, s):
        sign = 1 if way == 0 else -1
        ref = wfull.at[i, at_z(-sign * s)]
        if s == half:
            ref = ref.at[pl.ds(way * hc, hc)]
        remote(ref, ref, sem_w, (i, way, s - 1), to_z(-sign)).wait_recv()

    def w_step(s):
        for i in range(2):
            for way in range(2):
                if s > 1:
                    w_recv(i, way, s - 1)
                if s <= half:
                    w_copy(i, way, s).start()

    w_step(1)

    sums = jnp.zeros((t, cb), F32)
    for b in range(nz * NY):
        x = residual[:, b * cb : (b + 1) * cb].astype(F32)
        sums = sums + x * x
    inv_rms = lax.rsqrt(jnp.sum(sums, axis=1, keepdims=True) * (1.0 / c.d) + 1e-06)
    inv_ref[...] = jnp.broadcast_to(inv_rms, inv_ref.shape)
    for b in range(nz * NY):
        span = slice(b * cb, (b + 1) * cb)
        inner = slice((b // NY) * cb, (b // NY + 1) * cb)
        x = residual[:, span].astype(F32)
        tok_send[b % NY, :, inner] = (x * inv_rms * norm_gain[:, span]).astype(BF16)
        rw_slices[b % NY, :, inner] = router_weight[:, span]

    def tok_copy(d):
        return remote(tok_send.at[at_y(d)], tok.at[y], sem_tok, (d - 1,), to_y(d))

    for d in (2, 1, 3):
        tok_copy(d).start()

    logits = jnp.zeros((c.e, t), F32)
    for p in range(NY):
        logits = logits + nt(rw_slices[p], tok_send[p])
    top = jnp.max(logits, axis=0, keepdims=True)
    expo = jnp.exp(logits - top)
    probs = expo / jnp.sum(expo, axis=0, keepdims=True)
    expert_ids = lax.broadcasted_iota(jnp.int32, (c.e, t), 0)
    members = [(expert_ids == routes[k : k + 1, :]) for k in range(2)]
    counts = sum(jnp.where(mk, 1.0, 0.0) for mk in members)
    before = lax.broadcasted_iota(jnp.int32, (t, t), 0) < lax.broadcasted_iota(jnp.int32, (t, t), 1)
    ahead = nn(counts.astype(BF16), jnp.where(before, 1.0, 0.0).astype(BF16))
    prob_grad = jnp.zeros((c.e, t), F32)
    info[y] = jnp.zeros_like(info[y])
    for k in range(2):
        kept = keep[k : k + 1, :]
        prob_grad = prob_grad + jnp.where(members[k], kept.astype(F32) * gate[k : k + 1, :], 0.0)
        slot = jnp.sum(jnp.where(members[k], ahead, 0.0), axis=0, keepdims=True)
        route = routes[k : k + 1, :]
        base = (route & 1) * m + (route >> 1) * rows + y * cap
        row = jnp.where(kept == 1, base.astype(F32) + slot, -1.0)
        info[y, c.e + k : c.e + k + 1, :] = row
    logit_grad = (probs * (prob_grad - jnp.sum(probs * prob_grad, axis=0, keepdims=True))).astype(BF16)
    info[y, 0 : c.e, :] = logit_grad.astype(F32)

    def info_copy(d):
        return remote(info.at[y], info.at[y], sem_info, (d - 1,), to_y(d))

    for d in (2, 1, 3):
        info_copy(d).start()
    tok[y] = tok_send[y]
    w_step(2)
    for d in range(1, NY):
        ref = info.at[at_y(-d)]
        remote(ref, ref, sem_info, (d - 1,), to_y(-d)).wait_recv()
    for d in range(1, NY):
        ref = tok.at[at_y(-d)]
        remote(ref, ref, sem_tok, (d - 1,), to_y(-d)).wait_recv()

    def slot_copy(i, d):
        return remote(slots_out.at[i, at_x(d)], slots.at[i, me], sem_slot, (i, d - 1), to_x(d))

    def make_slots(i):
        targets = [
            jnp.concatenate([info[j, c.e + k : c.e + k + 1, :] for j in range(NY)], axis=1)
            for k in range(2)
        ]
        tokens = tok[...].reshape(NY * t, q)

        def place_rows(owner):
            row = lax.broadcasted_iota(jnp.int32, (rows, NY * t), 0) + (i * m + owner * rows)
            row = row.astype(F32)
            hit = (row == targets[0]) | (row == targets[1])
            placed = jnp.where(hit, 1.0, 0.0).astype(BF16)
            place[i, owner] = placed
            return nn(placed, tokens).astype(BF16)

        def step(d, carry):
            slots_out[i, at_x(d)] = place_rows(at_x(d))
            slot_copy(i, d).start()
            return carry

        lax.fori_loop(1, nx, step, 0)
        slots[i, me] = place_rows(me)

    make_slots(0)
    w_step(3)
    make_slots(1)
    for s in range(4, half + 1):
        w_step(s)

    lg_all = jnp.concatenate([info[j, 0 : c.e, :] for j in range(NY)], axis=1).astype(BF16)
    tokens = tok[...].reshape(NY * t, q)
    ar0[0 : c.e, :] = nn(lg_all, tokens)
    gain_acc[...] = jnp.zeros_like(gain_acc)
    for j in range(NY):
        back = tn(info[j, 0 : c.e, :].astype(BF16), rw_slices[y]) * tok[j].astype(F32)
        gain_acc[...] += jnp.sum(back.reshape(t // 8, 8, q), axis=0)

    def rs_copy(i, way, s):
        sign = 1 if way == 0 else -1
        if s == 0:
            src = part_perm.at[i, at_y(2), pl.ds(way * hb, hb)]
            dst = rs_a.at[i, way]
        else:
            src = part_perm.at[i, at_y(sign + NY)]
            dst = rs_b.at[i, way]
        return remote(src, dst, sem_rs, (i, way, s), to_y(sign + NY))

    def permuted(i, j):
        return nn(order[pl.ds(pl.multiple_of(j * blk, 16), blk), :], part[i])

    def preact_part(i):
        for s in range(half, half + 1):
            for way in range(2):
                w_recv(i, way, s)

        def wait_slots(d, carry):
            ref = slots.at[i, at_x(nx - d)]
            remote(ref, ref, sem_slot, (i, d - 1), to_x(nx - d)).wait_recv()
            return carry

        lax.fori_loop(1, nx, wait_slots, 0)

        def step(h, carry):
            some = slots[i, pl.ds(2 * h, 2)].reshape(2 * rows, q)
            wide = wfull[i].reshape(q, c.ff)
            part[i, pl.ds(pl.multiple_of(h * 2 * rows, 16), 2 * rows), :] = nn(some, wide).astype(BF16)
            return carry

        lax.fori_loop(0, nx // 2, step, 0)
        part_perm[i, at_y(2)] = permuted(i, at_y(2)).astype(BF16)
        for way in range(2):
            rs_copy(i, way, 0).start()

    def preact_relay(i):
        for way, sign in ((0, 1), (1, -1)):
            j = at_y(sign + NY)
            mine = permuted(i, j)
            ref = rs_a.at[i, way]
            remote(ref, ref, sem_rs, (i, way, 0), to_y(NY - sign)).wait_recv()
            span = slice(way * hb, (way + 1) * hb)
            other = slice((1 - way) * hb, (2 - way) * hb)
            part_perm[i, j, span] = (mine[span] + rs_a[i, way].astype(F32)).astype(BF16)
            part_perm[i, j, other] = mine[other].astype(BF16)
            rs_copy(i, way, 1).start()
        part_perm[i, y] = permuted(i, y).astype(BF16)

    def pg_copy(i, way, s):
        sign = 1 if way == 0 else -1
        if s == 0:
            ref = pre_grad.at[i, y]
        else:
            ref = pre_grad.at[i, at_y(NY - sign), pl.ds(way * hb, hb)]
        return remote(ref, ref, sem_pg, (i, way, s), to_y(sign + NY))

    def pg_recv(i, way, s):
        sign = 1 if way == 0 else -1
        if s == 0:
            ref = pre_grad.at[i, at_y(NY - sign)]
        else:
            ref = pre_grad.at[i, at_y(2), pl.ds(way * hb, hb)]
        remote(ref, ref, sem_pg, (i, way, s), to_y(NY - sign)).wait_recv()

    def make_pre_grad(i):
        for way, sign in ((0, 1), (1, -1)):
            ref = rs_b.at[i, way]
            remote(ref, ref, sem_rs, (i, way, 1), to_y(NY - sign)).wait_recv()
        preact = part_perm[i, y].astype(F32) + rs_b[i, 0].astype(F32) + rs_b[i, 1].astype(F32)
        pre_grad[i, y] = (grad_hidden[i].astype(F32) * silu_slope(preact)).astype(BF16)
        for way in range(2):
            pg_copy(i, way, 0).start()

    def relay_pre_grad(i):
        for way in range(2):
            pg_recv(i, way, 0)
            pg_copy(i, way, 1).start()

    def back_copy(i, d):
        return remote(backs.at[i, at_x(d)], returned.at[i, me], sem_back, (i, d - 1), to_x(d))

    def wg_copy(i, way, s):
        sign = 1 if way == 0 else -1
        src, dst = wg_out.at[i, way, s - 1], wg_in.at[i, way, s - 1]
        if s == 1:
            src, dst = src.at[pl.ds(way * hc, hc)], dst.at[pl.ds(way * hc, hc)]
        return remote(src, dst, sem_wg, (i, way, s - 1), to_z(sign))

    def wg_recv(i, way, s):
        sign = 1 if way == 0 else -1
        ref = wg_in.at[i, way, s - 1]
        if s == 1:
            ref = ref.at[pl.ds(way * hc, hc)]
        remote(ref, ref, sem_wg, (i, way, s - 1), to_z(-sign)).wait_recv()

    def weight_grad(i, owner):
        left = slots[i, :, :, pl.ds(pl.multiple_of(owner * cb, cb), cb)].reshape(m, cb)
        return tn(left, pg_rows[i])

    def wg_step(i, s):
        if s == 1:
            block = weight_grad(i, at_z(half)).astype(BF16)
            for way in range(2):
                span = slice(way * hc, (way + 1) * hc)
                wg_out[i, way, 0, span] = block[span]
                wg_copy(i, way, 1).start()
            return
        for way, sign in ((0, 1), (1, -1)):
            block = weight_grad(i, at_z(sign * (half + 1 - s)))
            wg_recv(i, way, s - 1)
            if s == 2:
                span = slice(way * hc, (way + 1) * hc)
                other = slice((1 - way) * hc, (2 - way) * hc)
                wg_out[i, way, 1, span] = (block[span] + wg_in[i, way, 0, span].astype(F32)).astype(BF16)
                wg_out[i, way, 1, other] = block[other].astype(BF16)
            else:
                wg_out[i, way, s - 1] = (block + wg_in[i, way, s - 2].astype(F32)).astype(BF16)
            wg_copy(i, way, s).start()

    def back_part(i):
        for way in range(2):
            pg_recv(i, way, 1)
        grads = pre_grad[i].reshape(m, c.ff)

        def unpermute(h, carry):
            span = pl.ds(pl.multiple_of(h * 2 * rows, 16), 2 * rows)
            pg_rows[i, span, :] = nn(order_t[span, :], grads).astype(BF16)
            return carry

        lax.fori_loop(0, nx // 2, unpermute, 0)
        wg_step(i, 1)

        def back_rows(owner):
            span = pl.ds(pl.multiple_of(owner * rows, 16), rows)
            out = nt(pg_rows[i, span, :], wfull[i].reshape(q, c.ff)).astype(BF16)
            terms = out.astype(F32) * slots[i, owner].astype(F32)
            gain_acc[...] += jnp.sum(terms.reshape(rows // 8, 8, q), axis=0)
            return out

        def step(d, carry):
            backs[i, at_x(d)] = back_rows(at_x(d))
            back_copy(i, d).start()
            return carry

        lax.fori_loop(1, nx, step, 0)
        returned[i, me] = back_rows(me)

    def combine(i):
        def wait_backs(d, carry):
            ref = returned.at[i, at_x(nx - d)]
            remote(ref, ref, sem_back, (i, d - 1), to_x(nx - d)).wait_recv()
            return carry

        lax.fori_loop(1, nx, wait_backs, 0)
        got = returned[i].reshape(m, q)
        for j in range(NY):
            there = place[i, :, :, j * t : (j + 1) * t].reshape(m, t)
            if i == 0:
                acc[j] = tn(there, got)
            else:
                tok_back[j] = (acc[j] + tn(there, got)).astype(BF16)

    preact_part(0)
    preact_part(1)
    preact_relay(0)
    preact_relay(1)
    make_pre_grad(0)
    make_pre_grad(1)
    relay_pre_grad(0)
    relay_pre_grad(1)
    back_part(0)
    back_part(1)

    ar0[c.e : c.e + 8, :] = gain_acc[...]

    def ar0_slice(e):
        return ar0.at[:, pl.ds(pl.multiple_of(e * cb, cb), cb)]

    def ar_x(d):
        return remote(ar0_slice(at_x(d)), ar1.at[me], sem_ar, (0, d - 1), to_x(d))

    for d in range(1, nx):
        ar_x(d).start()
    ar1[me] = ar0[:, pl.ds(pl.multiple_of(me * cb, cb), cb)]
    wg_step(0, 2)
    wg_step(1, 2)

    def wait_ar(index, ref, target):
        remote(ref, ref, sem_ar, index, target).wait_recv()

    for d in range(1, nx):
        wait_ar((0, d - 1), ar1.at[at_x(nx - d)], to_x(nx - d))
    ar2[z] = jnp.sum(ar1[...], axis=0)

    def ar_z(d):
        return remote(ar2.at[z], ar2.at[z], sem_ar, (1, d - 1), to_z(d))

    for d in range(1, nz):
        ar_z(d).start()
    wg_step(0, 3)
    wg_step(1, 3)
    for d in range(1, nz):
        wait_ar((1, d - 1), ar2.at[at_z(-d)], to_z(-d))
    ar3[y] = jnp.sum(ar2[...], axis=0)

    def ar_y(d):
        return remote(ar3.at[y], ar3.at[y], sem_ar, (2, d - 1), to_y(d))

    for d in range(1, NY):
        ar_y(d).start()
    combine(0)
    for s in range(4, half + 1):
        wg_step(0, s)
        wg_step(1, s)
    for d in range(1, NY):
        wait_ar((2, d - 1), ar3.at[at_y(NY - d)], to_y(NY - d))
    ar4[me] = ar3[...]

    def ar_out(d):
        return remote(ar3, ar4.at[me], sem_ar, (3, d - 1), to_x(d))

    for d in range(1, nx):
        ar_out(d).start()
    combine(1)

    def ret_copy(d):
        return remote(tok_back.at[at_y(d)], tok_ret.at[y], sem_ret, (d - 1,), to_y(d))

    for d in (2, 1, 3):
        ret_copy(d).start()
    tok_ret[y] = tok_back[y]

    for i in range(2):
        block = weight_grad(i, z)
        for way in range(2):
            wg_recv(i, way, half)
        up_out[i] = block + wg_in[i, 0, half - 1].astype(F32) + wg_in[i, 1, half - 1].astype(F32)

    for d in range(1, nx):
        wait_ar((3, d - 1), ar4.at[at_x(nx - d)], to_x(nx - d))
    for e in range(nx):
        for j in range(NY):
            span = slice((e * NY + j) * cb, (e * NY + j + 1) * cb)
            router_out[:, span] = ar4[e, j, 0 : c.e]
            total = jnp.sum(ar4[e, j, c.e : c.e + 8], axis=0, keepdims=True)
            gain_out[:, span] = total / norm_gain[:, span]

    for d in range(1, NY):
        ref = tok_ret.at[at_y(NY - d)]
        remote(ref, ref, sem_ret, (d - 1,), to_y(NY - d)).wait_recv()
    inv = inv_ref[...]
    grads = info[y, 0 : c.e, :].astype(BF16)
    inner = jnp.zeros((t, cb), F32)
    for p in range(NY):
        acc[p] = tn(grads, rw_slices[p]) + tok_ret[p].astype(F32)
    for b in range(nz * NY):
        span = slice(b * cb, (b + 1) * cb)
        here = slice((b // NY) * cb, (b // NY + 1) * cb)
        inner = inner + acc[b % NY, :, here] * norm_gain[:, span] * residual[:, span].astype(F32)
    mean = jnp.sum(inner, axis=1, keepdims=True) * (1.0 / c.d)
    scale = inv * inv * inv * mean
    for b in range(nz * NY):
        span = slice(b * cb, (b + 1) * cb)
        here = slice((b // NY) * cb, (b // NY + 1) * cb)
        scaled = acc[b % NY, :, here] * norm_gain[:, span]
        wide = residual[:, span].astype(F32)
        resid_out[:, span] = (inv * scaled - wide * scale).astype(BF16)

    for i in range(2):
        for way in range(2):
            for s in range(1, half + 1):
                w_copy(i, way, s).wait_send()
                wg_copy(i, way, s).wait_send()
            for s in range(2):
                rs_copy(i, way, s).wait_send()
                pg_copy(i, way, s).wait_send()
        for d in range(1, nx):
            slot_copy(i, d).wait_send()
            back_copy(i, d).wait_send()
    for d in range(1, NY):
        tok_copy(d).wait_send()
        info_copy(d).wait_send()
        ret_copy(d).wait_send()
        ar_y(d).wait_send()
    for d in range(1, nx):
        ar_x(d).wait_send()
        ar_out(d).wait_send()
    for d in range(1, nz):
        ar_z(d).wait_send()


def group_order(c):
    out = np.arange(c.m)
    group, sender, slot = out // c.blk, out % c.blk // c.cap, out % c.cap
    source = sender * c.rows + group * c.cap + slot
    table = np.zeros((c.m, c.m), np.float32)
    table[out, source] = 1.0
    return table


def local(
    mesh, residual, norm_gain, router_weight, up_weight, routes, keep_flags, gate_grad, grad_hidden
):
    c = Dims(
        mesh,
        residual.shape[0],
        residual.shape[1],
        up_weight.shape[2],
        grad_hidden.shape[1] // mesh.shape["expert"],
    )
    order = group_order(c)
    half = c.nz // 2
    dma = pltpu.SemaphoreType.DMA
    most = max(c.nz, c.nx) - 1
    vmem = pl.BlockSpec(memory_space=pltpu.VMEM)
    resid_grad, up_grad, router_grad, gain_grad = pl.pallas_call(
        functools.partial(kernel, c),
        out_shape=(
            jax.ShapeDtypeStruct((c.t, c.d), BF16),
            jax.ShapeDtypeStruct((2, c.cb, c.ff), F32),
            jax.ShapeDtypeStruct((c.e, c.d), F32),
            jax.ShapeDtypeStruct((1, c.d), F32),
        ),
        in_specs=[vmem] * 10,
        out_specs=(vmem,) * 4,
        scratch_shapes=[
            pltpu.VMEM((c.t, c.cb), F32),
            pltpu.VMEM((NY, c.t, c.q), BF16),
            pltpu.VMEM((NY, c.t, c.q), BF16),
            pltpu.VMEM((NY, c.e + 8, c.t), F32),
            pltpu.VMEM((NY, c.e, c.q), BF16),
            pltpu.VMEM((2, c.nx, c.rows, NY * c.t), BF16),
            pltpu.VMEM((2, c.nx, c.rows, c.q), BF16),
            pltpu.VMEM((2, c.nx, c.rows, c.q), BF16),
            pltpu.VMEM((2, c.nz, c.cb, c.ff), BF16),
            pltpu.VMEM((2, c.m, c.ff), BF16),
            pltpu.VMEM((2, NY, c.blk, c.ff), BF16),
            pltpu.VMEM((2, 2, c.blk // 2, c.ff), BF16),
            pltpu.VMEM((2, 2, c.blk, c.ff), BF16),
            pltpu.VMEM((2, NY, c.blk, c.ff), BF16),
            pltpu.VMEM((2, c.m, c.ff), BF16),
            pltpu.VMEM((2, c.nx, c.rows, c.q), BF16),
            pltpu.VMEM((2, c.nx, c.rows, c.q), BF16),
            pltpu.VMEM((2, 2, half, c.cb, c.ff), BF16),
            pltpu.VMEM((2, 2, half, c.cb, c.ff), BF16),
            pltpu.VMEM((NY, c.t, c.q), F32),
            pltpu.VMEM((NY, c.t, c.q), BF16),
            pltpu.VMEM((NY, c.t, c.q), BF16),
            pltpu.VMEM((8, c.q), F32),
            pltpu.VMEM((c.e + 8, c.q), F32),
            pltpu.VMEM((c.nx, c.e + 8, c.cb), F32),
            pltpu.VMEM((c.nz, c.e + 8, c.cb), F32),
            pltpu.VMEM((NY, c.e + 8, c.cb), F32),
            pltpu.VMEM((c.nx, NY, c.e + 8, c.cb), F32),
            dma((2, NY - 1)),
            dma((2, NY - 1)),
            dma((2, 2, c.nx - 1)),
            dma((2, 2, 2, half)),
            dma((2, 2, 2, 2)),
            dma((2, 2, 2, 2)),
            dma((2, 2, c.nx - 1)),
            dma((2, 2, 2, half)),
            dma((2, NY - 1)),
            dma((2, 4, most)),
        ],
        compiler_params=pltpu.CompilerParams(
            collective_id=0, has_side_effects=True, vmem_limit_bytes=60 * 2**20
        ),
        cost_estimate=pl.CostEstimate(
            flops=12 * c.m * c.q * c.ff, bytes_accessed=8 * 2**20, transcendentals=2 * c.blk * c.ff
        ),
    )(
        residual,
        norm_gain.reshape(1, c.d),
        router_weight,
        up_weight.transpose(1, 0, 2),
        routes.T,
        keep_flags.T,
        gate_grad.T,
        grad_hidden,
        jnp.asarray(order, BF16),
        jnp.asarray(order.T, BF16),
    )
    return (resid_grad, up_grad.transpose(1, 0, 2), router_grad, gain_grad.reshape(c.d))


def solution(mesh):
    in_specs = (
        P(("dp", "expert"), None),
        P(),
        P(),
        P("dp", "expert", None),
        P(("dp", "expert"), None),
        P(("dp", "expert"), None),
        P(("dp", "expert"), None),
        P("expert", "dp", None),
    )
    out_specs = (P(("dp", "expert"), None), P("dp", "expert", None), P(), P())
    return jax.shard_map(
        functools.partial(local, mesh), mesh=mesh, in_specs=in_specs, out_specs=out_specs, check_vma=False
    )
```

```python
import functools

import jax
import jax.numpy as jnp
import numpy as np
from jax import lax
from jax.experimental import pallas as pl
from jax.experimental.pallas import tpu as pltpu
from jax.sharding import PartitionSpec as P

NY = 4
BF16 = jnp.bfloat16
F32 = jnp.float32


def nn(a, b):
    return lax.dot_general(a, b, (((1,), (0,)), ((), ())), preferred_element_type=F32)


def nt(a, b):
    return lax.dot_general(a, b, (((1,), (1,)), ((), ())), preferred_element_type=F32)


def tn(a, b):
    return lax.dot_general(a, b, (((0,), (0,)), ((), ())), preferred_element_type=F32)


def silu_slope(v):
    s = jax.nn.sigmoid(v)
    return s * (1.0 + v * (1.0 - s))


class Dims:
    def __init__(self, mesh, tokens, width, ff, cap):
        self.nz = mesh.shape["dp"] // NY
        self.nx = mesh.shape["expert"]
        self.t = tokens
        self.d = width
        self.cb = width // (self.nz * NY)
        self.q = width // NY
        self.ff = ff
        self.cap = cap
        self.e = 2 * self.nx
        self.rows = NY * cap
        self.m = self.nx * self.rows
        self.blk = self.nx * cap


def kernel(
    c,
    residual,
    norm_gain,
    router_weight,
    weight,
    routes,
    keep,
    gate,
    grad_hidden_hbm,
    order_hbm,
    order_t_hbm,
    resid_out,
    up_out,
    router_out,
    gain_out,
    inv_ref,
    tok_send,
    tok,
    info,
    rw_slices,
    place,
    slots_out,
    slots,
    wfull,
    part,
    part_perm,
    rs_a,
    rs_b,
    pre_grad,
    pg_rows,
    backs,
    returned,
    wg_out,
    wg_in,
    acc,
    tok_back,
    tok_ret,
    gain_acc,
    ar0,
    ar1,
    ar2,
    ar3,
    ar4,
    sem_tok,
    sem_info,
    sem_slot,
    sem_w,
    sem_rs,
    sem_pg,
    sem_back,
    sem_wg,
    sem_ret,
    sem_ar,
    order,
    order_t,
    grad_hidden,
    sem_local,
):
    nz, nx, t, q, cb, cap, rows, m, blk = c.nz, c.nx, c.t, c.q, c.cb, c.cap, c.rows, c.m, c.blk
    half = nz // 2
    hq = q // 2
    hz = nz // 2
    hb = blk // 2
    hc = cb // 2
    dp = lax.axis_index("dp")
    me = lax.axis_index("expert")
    z, y = dp // NY, dp % NY

    def at_y(d):
        return (y + d) % NY

    def at_z(d):
        return (z + d + nz) % nz

    def at_x(d):
        return (me + d) % nx

    def to_y(d):
        return {"dp": z * NY + at_y(d)}

    def to_z(d):
        return {"dp": at_z(d) * NY + y}

    def to_x(d):
        return {"expert": at_x(d)}

    def remote(src, dst, sems, index, target):
        return pltpu.make_async_remote_copy(
            src_ref=src,
            dst_ref=dst,
            send_sem=sems.at[(0, *index)],
            recv_sem=sems.at[(1, *index)],
            device_id=target,
            device_id_type=pl.DeviceIdType.MESH,
        )

    late = [
        pltpu.make_async_copy(order_hbm, order, sem_local.at[0]),
        pltpu.make_async_copy(order_t_hbm, order_t, sem_local.at[1]),
        pltpu.make_async_copy(grad_hidden_hbm, grad_hidden, sem_local.at[2]),
    ]
    for copy in late:
        copy.start()

    barrier = pltpu.get_barrier_semaphore()
    for d in range(1, NY):
        pl.semaphore_signal(barrier, inc=1, device_id=to_y(d))
    for d in range(1, nz):
        pl.semaphore_signal(barrier, inc=1, device_id=to_z(d))
    for d in range(1, nx):
        pl.semaphore_signal(barrier, inc=1, device_id=to_x(d))
    pl.semaphore_wait(barrier, NY + nz + nx - 3)

    for i in range(2):
        wfull[i, z] = weight[i]

    def w_copy(i, way, s):
        sign = 1 if way == 0 else -1
        source = at_z(-sign * (s - 1))
        ref = wfull.at[i, source]
        if s == half:
            ref = ref.at[pl.ds(way * hc, hc)]
        return remote(ref, ref, sem_w, (i, way, s - 1), to_z(sign))

    def w_recv(i, way, s):
        sign = 1 if way == 0 else -1
        ref = wfull.at[i, at_z(-sign * s)]
        if s == half:
            ref = ref.at[pl.ds(way * hc, hc)]
        remote(ref, ref, sem_w, (i, way, s - 1), to_z(-sign)).wait_recv()

    def w_step(s):
        for i in range(2):
            for way in range(2):
                if s > 1:
                    w_recv(i, way, s - 1)
                if s <= half:
                    w_copy(i, way, s).start()

    w_step(1)

    sums = jnp.zeros((t, cb), F32)
    for b in range(nz * NY):
        x = residual[:, b * cb : (b + 1) * cb].astype(F32)
        sums = sums + x * x
    inv_rms = lax.rsqrt(jnp.sum(sums, axis=1, keepdims=True) * (1.0 / c.d) + 1e-06)
    inv_ref[...] = jnp.broadcast_to(inv_rms, inv_ref.shape)

    def norm_slice(h, p):
        for b in range(hz):
            span = pl.ds(pl.multiple_of(((h * hz + b) * NY + p) * cb, cb), cb)
            x = residual[:, span].astype(F32)
            tok_send[h, p, :, b * cb : (b + 1) * cb] = (x * inv_rms * norm_gain[:, span]).astype(BF16)

    def tok_copy(h, d):
        return remote(tok_send.at[h, at_y(d)], tok.at[h, y], sem_tok, (h, d - 1), to_y(d))

    for d in (2, 1, 3):
        norm_slice(0, at_y(d))
        tok_copy(0, d).start()
    norm_slice(0, y)
    for p in range(NY):
        norm_slice(1, p)
    for b in range(nz * NY):
        inner = slice((b // NY) * cb, (b // NY + 1) * cb)
        rw_slices[b % NY, :, inner] = router_weight[:, b * cb : (b + 1) * cb]

    logits = jnp.zeros((c.e, t), F32)
    for p in range(NY):
        for h in range(2):
            logits = logits + nt(rw_slices[p, :, h * hq : (h + 1) * hq], tok_send[h, p])
    top = jnp.max(logits, axis=0, keepdims=True)
    expo = jnp.exp(logits - top)
    probs = expo / jnp.sum(expo, axis=0, keepdims=True)
    expert_ids = lax.broadcasted_iota(jnp.int32, (c.e, t), 0)
    members = [(expert_ids == routes[k : k + 1, :]) for k in range(2)]
    counts = sum(jnp.where(mk, 1.0, 0.0) for mk in members)
    before = lax.broadcasted_iota(jnp.int32, (t, t), 0) < lax.broadcasted_iota(jnp.int32, (t, t), 1)
    ahead = nn(counts.astype(BF16), jnp.where(before, 1.0, 0.0).astype(BF16))
    prob_grad = jnp.zeros((c.e, t), F32)
    info[y] = jnp.zeros_like(info[y])
    for k in range(2):
        kept = keep[k : k + 1, :]
        prob_grad = prob_grad + jnp.where(members[k], kept.astype(F32) * gate[k : k + 1, :], 0.0)
        slot = jnp.sum(jnp.where(members[k], ahead, 0.0), axis=0, keepdims=True)
        route = routes[k : k + 1, :]
        base = (route & 1) * m + (route >> 1) * rows + y * cap
        row = jnp.where(kept == 1, base.astype(F32) + slot, -1.0)
        info[y, c.e + k : c.e + k + 1, :] = row
    logit_grad = (probs * (prob_grad - jnp.sum(probs * prob_grad, axis=0, keepdims=True))).astype(BF16)
    info[y, 0 : c.e, :] = logit_grad.astype(F32)

    def info_copy(d):
        return remote(info.at[y], info.at[y], sem_info, (d - 1,), to_y(d))

    for d in (2, 1, 3):
        info_copy(d).start()
    for d in (2, 1, 3):
        tok_copy(1, d).start()
    for h in range(2):
        tok[h, y] = tok_send[h, y]
    w_step(2)
    for d in range(1, NY):
        ref = info.at[at_y(-d)]
        remote(ref, ref, sem_info, (d - 1,), to_y(-d)).wait_recv()

    def wait_tok(h):
        for d in range(1, NY):
            ref = tok.at[h, at_y(-d)]
            remote(ref, ref, sem_tok, (h, d - 1), to_y(-d)).wait_recv()

    def slot_copy(i, h, d):
        return remote(slots_out.at[i, h, at_x(d)], slots.at[i, h, me], sem_slot, (i, h, d - 1), to_x(d))

    def make_slots(i, h):
        targets = [
            jnp.concatenate([info[j, c.e + k : c.e + k + 1, :] for j in range(NY)], axis=1)
            for k in range(2)
        ]
        tokens = tok[h].reshape(NY * t, hq)

        def slot_rows(owner):
            if h == 0:
                row = lax.broadcasted_iota(jnp.int32, (rows, NY * t), 0) + (i * m + owner * rows)
                row = row.astype(F32)
                hit = (row == targets[0]) | (row == targets[1])
                place[i, owner] = jnp.where(hit, 1.0, 0.0).astype(BF16)
            return nn(place[i, owner], tokens).astype(BF16)

        def step(d, carry):
            slots_out[i, h, at_x(d)] = slot_rows(at_x(d))
            slot_copy(i, h, d).start()
            return carry

        lax.fori_loop(1, nx, step, 0)
        slots[i, h, me] = slot_rows(me)

    wait_tok(0)
    make_slots(0, 0)
    wait_tok(1)
    make_slots(0, 1)
    make_slots(1, 0)
    make_slots(1, 1)
    for s in range(3, half + 1):
        w_step(s)

    lg_all = jnp.concatenate([info[j, 0 : c.e, :] for j in range(NY)], axis=1).astype(BF16)
    for h in range(2):
        span = slice(h * hq, (h + 1) * hq)
        ar0[0 : c.e, span] = nn(lg_all, tok[h].reshape(NY * t, hq))
        total = jnp.zeros((8, hq), F32)
        for j in range(NY):
            back = tn(info[j, 0 : c.e, :].astype(BF16), rw_slices[y, :, span]) * tok[h, j].astype(F32)
            total = total + jnp.sum(back.reshape(t // 8, 8, hq), axis=0)
        gain_acc[:, span] = total
    for copy in late:
        copy.wait()

    def rs_copy(i, way, s):
        sign = 1 if way == 0 else -1
        if s == 0:
            src = part_perm.at[i, at_y(2), pl.ds(way * hb, hb)]
            dst = rs_a.at[i, way]
        else:
            src = part_perm.at[i, at_y(sign + NY)]
            dst = rs_b.at[i, way]
        return remote(src, dst, sem_rs, (i, way, s), to_y(sign + NY))

    def permuted(i, j):
        return nn(order[pl.ds(pl.multiple_of(j * blk, 16), blk), :], part[i])

    def preact_part(i):
        for s in range(half, half + 1):
            for way in range(2):
                w_recv(i, way, s)

        def wait_slots(d, carry):
            for h in range(2):
                ref = slots.at[i, h, at_x(nx - d)]
                remote(ref, ref, sem_slot, (i, h, d - 1), to_x(nx - d)).wait_recv()
            return carry

        lax.fori_loop(1, nx, wait_slots, 0)

        def step(h, carry):
            total = jnp.zeros((2 * rows, c.ff), F32)
            for side in range(2):
                some = slots[i, side, pl.ds(2 * h, 2)].reshape(2 * rows, hq)
                total = total + nn(some, wfull[i, side * hz : (side + 1) * hz].reshape(hq, c.ff))
            part[i, pl.ds(pl.multiple_of(h * 2 * rows, 16), 2 * rows), :] = total.astype(BF16)
            return carry

        lax.fori_loop(0, nx // 2, step, 0)
        part_perm[i, at_y(2)] = permuted(i, at_y(2)).astype(BF16)
        for way in range(2):
            rs_copy(i, way, 0).start()

    def preact_relay(i):
        for way, sign in ((0, 1), (1, -1)):
            j = at_y(sign + NY)
            mine = permuted(i, j)
            ref = rs_a.at[i, way]
            remote(ref, ref, sem_rs, (i, way, 0), to_y(NY - sign)).wait_recv()
            span = slice(way * hb, (way + 1) * hb)
            other = slice((1 - way) * hb, (2 - way) * hb)
            part_perm[i, j, span] = (mine[span] + rs_a[i, way].astype(F32)).astype(BF16)
            part_perm[i, j, other] = mine[other].astype(BF16)
            rs_copy(i, way, 1).start()
        part_perm[i, y] = permuted(i, y).astype(BF16)

    def pg_copy(i, way, s):
        sign = 1 if way == 0 else -1
        if s == 0:
            ref = pre_grad.at[i, y]
        else:
            ref = pre_grad.at[i, at_y(NY - sign), pl.ds(way * hb, hb)]
        return remote(ref, ref, sem_pg, (i, way, s), to_y(sign + NY))

    def pg_recv(i, way, s):
        sign = 1 if way == 0 else -1
        if s == 0:
            ref = pre_grad.at[i, at_y(NY - sign)]
        else:
            ref = pre_grad.at[i, at_y(2), pl.ds(way * hb, hb)]
        remote(ref, ref, sem_pg, (i, way, s), to_y(NY - sign)).wait_recv()

    def make_pre_grad(i):
        for way, sign in ((0, 1), (1, -1)):
            ref = rs_b.at[i, way]
            remote(ref, ref, sem_rs, (i, way, 1), to_y(NY - sign)).wait_recv()
        preact = part_perm[i, y].astype(F32) + rs_b[i, 0].astype(F32) + rs_b[i, 1].astype(F32)
        pre_grad[i, y] = (grad_hidden[i].astype(F32) * silu_slope(preact)).astype(BF16)
        for way in range(2):
            pg_copy(i, way, 0).start()

    def relay_pre_grad(i):
        for way in range(2):
            pg_recv(i, way, 0)
            pg_copy(i, way, 1).start()

    def back_copy(i, h, d):
        return remote(backs.at[i, h, at_x(d)], returned.at[i, h, me], sem_back, (i, h, d - 1), to_x(d))

    def wg_copy(i, way, s):
        sign = 1 if way == 0 else -1
        src, dst = wg_out.at[i, way, s - 1], wg_in.at[i, way, s - 1]
        if s == 1:
            src, dst = src.at[pl.ds(way * hc, hc)], dst.at[pl.ds(way * hc, hc)]
        return remote(src, dst, sem_wg, (i, way, s - 1), to_z(sign))

    def wg_recv(i, way, s):
        sign = 1 if way == 0 else -1
        ref = wg_in.at[i, way, s - 1]
        if s == 1:
            ref = ref.at[pl.ds(way * hc, hc)]
        remote(ref, ref, sem_wg, (i, way, s - 1), to_z(-sign)).wait_recv()

    def weight_grad(i, owner):
        inside = pl.ds(pl.multiple_of((owner % hz) * cb, cb), cb)
        left = slots[i, owner // hz, :, :, inside].reshape(m, cb)
        return tn(left, pg_rows[i])

    def wg_step(i, s):
        if s == 1:
            block = weight_grad(i, at_z(half)).astype(BF16)
            for way in range(2):
                span = slice(way * hc, (way + 1) * hc)
                wg_out[i, way, 0, span] = block[span]
                wg_copy(i, way, 1).start()
            return
        for way, sign in ((0, 1), (1, -1)):
            block = weight_grad(i, at_z(sign * (half + 1 - s)))
            wg_recv(i, way, s - 1)
            if s == 2:
                span = slice(way * hc, (way + 1) * hc)
                other = slice((1 - way) * hc, (2 - way) * hc)
                wg_out[i, way, 1, span] = (block[span] + wg_in[i, way, 0, span].astype(F32)).astype(BF16)
                wg_out[i, way, 1, other] = block[other].astype(BF16)
            else:
                wg_out[i, way, s - 1] = (block + wg_in[i, way, s - 2].astype(F32)).astype(BF16)
            wg_copy(i, way, s).start()

    def back_part(i):
        for way in range(2):
            pg_recv(i, way, 1)
        grads = pre_grad[i].reshape(m, c.ff)

        def unpermute(h, carry):
            span = pl.ds(pl.multiple_of(h * 2 * rows, 16), 2 * rows)
            pg_rows[i, span, :] = nn(order_t[span, :], grads).astype(BF16)
            return carry

        lax.fori_loop(0, nx // 2, unpermute, 0)
        wide = 2 * cb
        for h in range(2):
            for b in range(hq // wide):
                span = slice(b * wide, (b + 1) * wide)
                first = h * hz + 2 * b
                out = nt(pg_rows[i], wfull[i, first : first + 2].reshape(wide, c.ff)).astype(BF16)
                backs[i, h, :, :, span] = out.reshape(nx, rows, wide)
                terms = out.astype(F32) * slots[i, h, :, :, span].reshape(m, wide).astype(F32)
                where = slice(h * hq + b * wide, h * hq + (b + 1) * wide)
                gain_acc[:, where] += jnp.sum(terms.reshape(m // 8, 8, wide), axis=0)
            if i == 0:
                send_backs(i, h)
            if h == 0:
                wg_step(i, 1)

    def send_backs(i, h):
        def step(d, carry):
            back_copy(i, h, d).start()
            return carry

        lax.fori_loop(1, nx, step, 0)
        returned[i, h, me] = backs[i, h, me]

    def combine(i, h):
        def wait_backs(d, carry):
            ref = returned.at[i, h, at_x(nx - d)]
            remote(ref, ref, sem_back, (i, h, d - 1), to_x(nx - d)).wait_recv()
            return carry

        lax.fori_loop(1, nx, wait_backs, 0)
        got = returned[i, h].reshape(m, hq)
        span = slice(h * hq, (h + 1) * hq)
        for j in range(NY):
            there = place[i, :, :, j * t : (j + 1) * t].reshape(m, t)
            if i == 0:
                acc[j, :, span] = tn(there, got)
            else:
                tok_back[h, j] = (acc[j, :, span] + tn(there, got)).astype(BF16)

    def ret_copy(h, d):
        return remote(tok_back.at[h, at_y(d)], tok_ret.at[h, y], sem_ret, (h, d - 1), to_y(d))

    def send_ret(h):
        for d in (2, 1, 3):
            ret_copy(h, d).start()
        tok_ret[h, y] = tok_back[h, y]

    preact_part(0)
    preact_relay(0)
    preact_part(1)
    make_pre_grad(0)
    preact_relay(1)
    relay_pre_grad(0)
    make_pre_grad(1)
    back_part(0)
    relay_pre_grad(1)
    back_part(1)

    ar0[c.e : c.e + 8, :] = gain_acc[...]

    def ar0_slice(e):
        return ar0.at[:, pl.ds(pl.multiple_of(e * cb, cb), cb)]

    def ar_x(d):
        return remote(ar0_slice(at_x(d)), ar1.at[me], sem_ar, (0, d - 1), to_x(d))

    for d in range(1, nx):
        ar_x(d).start()
    send_backs(1, 0)
    send_backs(1, 1)
    ar1[me] = ar0[:, pl.ds(pl.multiple_of(me * cb, cb), cb)]
    wg_step(0, 2)
    wg_step(1, 2)

    def wait_ar(index, ref, target):
        remote(ref, ref, sem_ar, index, target).wait_recv()

    for d in range(1, nx):
        wait_ar((0, d - 1), ar1.at[at_x(nx - d)], to_x(nx - d))
    ar2[z] = jnp.sum(ar1[...], axis=0)

    def ar_z(d):
        return remote(ar2.at[z], ar2.at[z], sem_ar, (1, d - 1), to_z(d))

    for d in range(1, nz):
        ar_z(d).start()
    wg_step(0, 3)
    wg_step(1, 3)
    for d in range(1, nz):
        wait_ar((1, d - 1), ar2.at[at_z(-d)], to_z(-d))
    ar3[y] = jnp.sum(ar2[...], axis=0)

    def ar_y(d):
        return remote(ar3.at[y], ar3.at[y], sem_ar, (2, d - 1), to_y(d))

    for d in range(1, NY):
        ar_y(d).start()
    for h in range(2):
        combine(0, h)
    for s in range(4, half + 1):
        wg_step(0, s)
        wg_step(1, s)
    for d in range(1, NY):
        wait_ar((2, d - 1), ar3.at[at_y(NY - d)], to_y(NY - d))
    ar4[me] = ar3[...]

    def ar_out(d):
        return remote(ar3, ar4.at[me], sem_ar, (3, d - 1), to_x(d))

    for d in range(1, nx):
        ar_out(d).start()
    for h in range(2):
        combine(1, h)
        send_ret(h)

    for i in range(2):
        block = weight_grad(i, z)
        for way in range(2):
            wg_recv(i, way, half)
        up_out[:, i, :] = block + wg_in[i, 0, half - 1].astype(F32) + wg_in[i, 1, half - 1].astype(F32)

    for d in range(1, nx):
        wait_ar((3, d - 1), ar4.at[at_x(nx - d)], to_x(nx - d))
    for e in range(nx):
        for j in range(NY):
            span = slice((e * NY + j) * cb, (e * NY + j + 1) * cb)
            router_out[:, span] = ar4[e, j, 0 : c.e]
            total = jnp.sum(ar4[e, j, c.e : c.e + 8], axis=0, keepdims=True)
            gain_out[:, span] = total / norm_gain[:, span]

    inv = inv_ref[...]
    grads = info[y, 0 : c.e, :].astype(BF16)
    inner = jnp.zeros((t, cb), F32)
    for h in range(2):
        for d in range(1, NY):
            ref = tok_ret.at[h, at_y(NY - d)]
            remote(ref, ref, sem_ret, (h, d - 1), to_y(NY - d)).wait_recv()
        for p in range(NY):
            half_span = slice(h * hq, (h + 1) * hq)
            acc[p, :, half_span] = tn(grads, rw_slices[p, :, half_span]) + tok_ret[h, p].astype(F32)
        for b in range(h * hz * NY, (h + 1) * hz * NY):
            span = slice(b * cb, (b + 1) * cb)
            here = slice((b // NY) * cb, (b // NY + 1) * cb)
            inner = inner + acc[b % NY, :, here] * norm_gain[:, span] * residual[:, span].astype(F32)
    mean = jnp.sum(inner, axis=1, keepdims=True) * (1.0 / c.d)
    scale = inv * inv * inv * mean
    for b in range(nz * NY):
        span = slice(b * cb, (b + 1) * cb)
        here = slice((b // NY) * cb, (b // NY + 1) * cb)
        scaled = acc[b % NY, :, here] * norm_gain[:, span]
        wide = residual[:, span].astype(F32)
        resid_out[:, span] = (inv * scaled - wide * scale).astype(BF16)

    for i in range(2):
        for way in range(2):
            for s in range(1, half + 1):
                w_copy(i, way, s).wait_send()
                wg_copy(i, way, s).wait_send()
            for s in range(2):
                rs_copy(i, way, s).wait_send()
                pg_copy(i, way, s).wait_send()
        for h in range(2):
            for d in range(1, nx):
                slot_copy(i, h, d).wait_send()
                back_copy(i, h, d).wait_send()
    for d in range(1, NY):
        for h in range(2):
            tok_copy(h, d).wait_send()
            ret_copy(h, d).wait_send()
        info_copy(d).wait_send()
        ar_y(d).wait_send()
    for d in range(1, nx):
        ar_x(d).wait_send()
        ar_out(d).wait_send()
    for d in range(1, nz):
        ar_z(d).wait_send()


def group_order(c):
    out = np.arange(c.m)
    group, sender, slot = out // c.blk, out % c.blk // c.cap, out % c.cap
    source = sender * c.rows + group * c.cap + slot
    table = np.zeros((c.m, c.m), np.float32)
    table[out, source] = 1.0
    return table


def local(
    mesh, residual, norm_gain, router_weight, up_weight, routes, keep_flags, gate_grad, grad_hidden
):
    c = Dims(
        mesh,
        residual.shape[0],
        residual.shape[1],
        up_weight.shape[2],
        grad_hidden.shape[1] // mesh.shape["expert"],
    )
    order = group_order(c)
    half = c.nz // 2
    dma = pltpu.SemaphoreType.DMA
    most = max(c.nz, c.nx) - 1
    vmem = pl.BlockSpec(memory_space=pltpu.VMEM)
    resid_grad, up_grad, router_grad, gain_grad = pl.pallas_call(
        functools.partial(kernel, c),
        out_shape=(
            jax.ShapeDtypeStruct((c.t, c.d), BF16),
            jax.ShapeDtypeStruct((c.cb, 2, c.ff), F32),
            jax.ShapeDtypeStruct((c.e, c.d), F32),
            jax.ShapeDtypeStruct((1, c.d), F32),
        ),
        in_specs=[vmem] * 7 + [pl.BlockSpec(memory_space=pl.ANY)] * 3,
        out_specs=(vmem,) * 4,
        scratch_shapes=[
            pltpu.VMEM((c.t, c.cb), F32),
            pltpu.VMEM((2, NY, c.t, c.q // 2), BF16),
            pltpu.VMEM((2, NY, c.t, c.q // 2), BF16),
            pltpu.VMEM((NY, c.e + 8, c.t), F32),
            pltpu.VMEM((NY, c.e, c.q), BF16),
            pltpu.VMEM((2, c.nx, c.rows, NY * c.t), BF16),
            pltpu.VMEM((2, 2, c.nx, c.rows, c.q // 2), BF16),
            pltpu.VMEM((2, 2, c.nx, c.rows, c.q // 2), BF16),
            pltpu.VMEM((2, c.nz, c.cb, c.ff), BF16),
            pltpu.VMEM((2, c.m, c.ff), BF16),
            pltpu.VMEM((2, NY, c.blk, c.ff), BF16),
            pltpu.VMEM((2, 2, c.blk // 2, c.ff), BF16),
            pltpu.VMEM((2, 2, c.blk, c.ff), BF16),
            pltpu.VMEM((2, NY, c.blk, c.ff), BF16),
            pltpu.VMEM((2, c.m, c.ff), BF16),
            pltpu.VMEM((2, 2, c.nx, c.rows, c.q // 2), BF16),
            pltpu.VMEM((2, 2, c.nx, c.rows, c.q // 2), BF16),
            pltpu.VMEM((2, 2, half, c.cb, c.ff), BF16),
            pltpu.VMEM((2, 2, half, c.cb, c.ff), BF16),
            pltpu.VMEM((NY, c.t, c.q), F32),
            pltpu.VMEM((2, NY, c.t, c.q // 2), BF16),
            pltpu.VMEM((2, NY, c.t, c.q // 2), BF16),
            pltpu.VMEM((8, c.q), F32),
            pltpu.VMEM((c.e + 8, c.q), F32),
            pltpu.VMEM((c.nx, c.e + 8, c.cb), F32),
            pltpu.VMEM((c.nz, c.e + 8, c.cb), F32),
            pltpu.VMEM((NY, c.e + 8, c.cb), F32),
            pltpu.VMEM((c.nx, NY, c.e + 8, c.cb), F32),
            dma((2, 2, NY - 1)),
            dma((2, NY - 1)),
            dma((2, 2, 2, c.nx - 1)),
            dma((2, 2, 2, half)),
            dma((2, 2, 2, 2)),
            dma((2, 2, 2, 2)),
            dma((2, 2, 2, c.nx - 1)),
            dma((2, 2, 2, half)),
            dma((2, 2, NY - 1)),
            dma((2, 4, most)),
            pltpu.VMEM((c.m, c.m), BF16),
            pltpu.VMEM((c.m, c.m), BF16),
            pltpu.VMEM((2, c.blk, c.ff), BF16),
            dma((3,)),
        ],
        compiler_params=pltpu.CompilerParams(
            collective_id=0, has_side_effects=True, vmem_limit_bytes=60 * 2**20
        ),
        cost_estimate=pl.CostEstimate(
            flops=12 * c.m * c.q * c.ff, bytes_accessed=8 * 2**20, transcendentals=2 * c.blk * c.ff
        ),
    )(
        residual,
        norm_gain.reshape(1, c.d),
        router_weight,
        up_weight.transpose(1, 0, 2),
        routes.T,
        keep_flags.T,
        gate_grad.T,
        grad_hidden,
        jnp.asarray(order, BF16),
        jnp.asarray(order.T, BF16),
    )
    return (resid_grad, up_grad, router_grad, gain_grad.reshape(c.d))


def solution(mesh):
    in_specs = (
        P(("dp", "expert"), None),
        P(),
        P(),
        P("dp", "expert", None),
        P(("dp", "expert"), None),
        P(("dp", "expert"), None),
        P(("dp", "expert"), None),
        P("expert", "dp", None),
    )
    out_specs = (P(("dp", "expert"), None), P("dp", "expert", None), P(), P())
    return jax.shard_map(
        functools.partial(local, mesh), mesh=mesh, in_specs=in_specs, out_specs=out_specs, check_vma=False
    )
```

```python
import functools

import jax
import jax.numpy as jnp
import numpy as np
from jax import lax
from jax.experimental import pallas as pl
from jax.experimental.pallas import tpu as pltpu
from jax.sharding import PartitionSpec as P

NY = 4
BF16 = jnp.bfloat16
F32 = jnp.float32


def nn(a, b):
    return lax.dot_general(a, b, (((1,), (0,)), ((), ())), preferred_element_type=F32)


def nt(a, b):
    return lax.dot_general(a, b, (((1,), (1,)), ((), ())), preferred_element_type=F32)


def tn(a, b):
    return lax.dot_general(a, b, (((0,), (0,)), ((), ())), preferred_element_type=F32)


def silu_slope(v):
    s = jax.nn.sigmoid(v)
    return s * (1.0 + v * (1.0 - s))


class Dims:
    def __init__(self, mesh, tokens, width, ff, cap):
        self.nz = mesh.shape["dp"] // NY
        self.nx = mesh.shape["expert"]
        self.t = tokens
        self.d = width
        self.cb = width // (self.nz * NY)
        self.q = width // NY
        self.ff = ff
        self.cap = cap
        self.e = 2 * self.nx
        self.rows = NY * cap
        self.m = self.nx * self.rows
        self.blk = self.nx * cap


def kernel(
    c,
    residual_hbm,
    norm_gain,
    router_weight,
    weight_hbm,
    routes,
    keep,
    gate,
    grad_hidden_hbm,
    order_hbm,
    order_t_hbm,
    resid_out,
    up_out,
    router_out,
    gain_out,
    inv_ref,
    tok_send,
    tok,
    info,
    rw_slices,
    place,
    slots_out,
    slots,
    wfull,
    part,
    part_perm,
    rs_a,
    rs_b,
    pre_grad,
    pg_rows,
    backs,
    returned,
    wg_out,
    wg_in,
    acc,
    tok_back,
    tok_ret,
    gain_acc,
    ar0,
    ar1,
    ar2,
    ar3,
    ar4,
    sem_tok,
    sem_info,
    sem_slot,
    sem_w,
    sem_rs,
    sem_pg,
    sem_back,
    sem_wg,
    sem_ret,
    sem_ar,
    order,
    order_t,
    grad_hidden,
    residual,
    wg_own,
    sem_local,
):
    nz, nx, t, q, cb, cap, rows, m, blk = c.nz, c.nx, c.t, c.q, c.cb, c.cap, c.rows, c.m, c.blk
    half = nz // 2
    hq = q // 2
    hz = nz // 2
    hb = blk // 2
    hc = cb // 2
    dp = lax.axis_index("dp")
    me = lax.axis_index("expert")
    z, y = dp // NY, dp % NY

    def at_y(d):
        return (y + d) % NY

    def at_z(d):
        return (z + d + nz) % nz

    def at_x(d):
        return (me + d) % nx

    def to_y(d):
        return {"dp": z * NY + at_y(d)}

    def to_z(d):
        return {"dp": at_z(d) * NY + y}

    def to_x(d):
        return {"expert": at_x(d)}

    def remote(src, dst, sems, index, target):
        return pltpu.make_async_remote_copy(
            src_ref=src,
            dst_ref=dst,
            send_sem=sems.at[(0, *index)],
            recv_sem=sems.at[(1, *index)],
            device_id=target,
            device_id_type=pl.DeviceIdType.MESH,
        )

    early = [
        pltpu.make_async_copy(weight_hbm.at[0], wfull.at[0, z], sem_local.at[3]),
        pltpu.make_async_copy(weight_hbm.at[1], wfull.at[1, z], sem_local.at[4]),
        pltpu.make_async_copy(residual_hbm, residual, sem_local.at[5]),
    ]
    for copy in early:
        copy.start()
    late = [
        pltpu.make_async_copy(order_hbm, order, sem_local.at[0]),
        pltpu.make_async_copy(order_t_hbm, order_t, sem_local.at[1]),
        pltpu.make_async_copy(grad_hidden_hbm, grad_hidden, sem_local.at[2]),
    ]
    barrier = pltpu.get_barrier_semaphore()
    for d in range(1, NY):
        pl.semaphore_signal(barrier, inc=1, device_id=to_y(d))
    for d in range(1, nz):
        pl.semaphore_signal(barrier, inc=1, device_id=to_z(d))
    for d in range(1, nx):
        pl.semaphore_signal(barrier, inc=1, device_id=to_x(d))
    pl.semaphore_wait(barrier, NY + nz + nx - 3)

    def w_piece(i, way, s, piece, source):
        sign = 1 if way == 0 else -1
        ref = wfull.at[i, source, pl.ds(piece * hc, hc)]
        return remote(ref, ref, sem_w, (i, way, s - 1, piece), to_z(sign))

    def w_copy(i, way, s, piece):
        sign = 1 if way == 0 else -1
        return w_piece(i, way, s, piece, at_z(-sign * (s - 1)))

    def w_recv(i, way, s, piece):
        sign = 1 if way == 0 else -1
        w_piece(i, way, s, piece, at_z(-sign * s)).wait_recv()

    def w_step(i, s, piece):
        for way in range(2):
            if s > 1:
                w_recv(i, way, s - 1, piece)
            if s < half or way == piece:
                w_copy(i, way, s, piece).start()

    early[0].wait()
    w_step(0, 1, 0)
    w_step(0, 1, 1)
    early[1].wait()
    early[2].wait()
    for copy in late:
        copy.start()

    sums = jnp.zeros((t, cb), F32)
    for b in range(nz * NY):
        x = residual[:, b * cb : (b + 1) * cb].astype(F32)
        sums = sums + x * x
    inv_rms = lax.rsqrt(jnp.sum(sums, axis=1, keepdims=True) * (1.0 / c.d) + 1e-06)
    inv_ref[...] = jnp.broadcast_to(inv_rms, inv_ref.shape)

    def norm_slice(h, p):
        for b in range(hz):
            span = pl.ds(pl.multiple_of(((h * hz + b) * NY + p) * cb, cb), cb)
            x = residual[:, span].astype(F32)
            tok_send[h, p, :, b * cb : (b + 1) * cb] = (x * inv_rms * norm_gain[:, span]).astype(BF16)

    def tok_copy(h, d):
        return remote(tok_send.at[h, at_y(d)], tok.at[h, y], sem_tok, (h, d - 1), to_y(d))

    for d in (2, 1, 3):
        norm_slice(0, at_y(d))
        tok_copy(0, d).start()
    norm_slice(0, y)
    w_step(0, 2, 0)
    for p in range(NY):
        norm_slice(1, p)
    for b in range(nz * NY):
        inner = slice((b // NY) * cb, (b // NY + 1) * cb)
        rw_slices[b % NY, :, inner] = router_weight[:, b * cb : (b + 1) * cb]

    logits = jnp.zeros((c.e, t), F32)
    for p in range(NY):
        for h in range(2):
            logits = logits + nt(rw_slices[p, :, h * hq : (h + 1) * hq], tok_send[h, p])
    top = jnp.max(logits, axis=0, keepdims=True)
    expo = jnp.exp(logits - top)
    probs = expo / jnp.sum(expo, axis=0, keepdims=True)
    expert_ids = lax.broadcasted_iota(jnp.int32, (c.e, t), 0)
    members = [(expert_ids == routes[k : k + 1, :]) for k in range(2)]
    counts = sum(jnp.where(mk, 1.0, 0.0) for mk in members)
    before = lax.broadcasted_iota(jnp.int32, (t, t), 0) < lax.broadcasted_iota(jnp.int32, (t, t), 1)
    ahead = nn(counts.astype(BF16), jnp.where(before, 1.0, 0.0).astype(BF16))
    prob_grad = jnp.zeros((c.e, t), F32)
    info[y] = jnp.zeros_like(info[y])
    for k in range(2):
        kept = keep[k : k + 1, :]
        prob_grad = prob_grad + jnp.where(members[k], kept.astype(F32) * gate[k : k + 1, :], 0.0)
        slot = jnp.sum(jnp.where(members[k], ahead, 0.0), axis=0, keepdims=True)
        route = routes[k : k + 1, :]
        base = (route & 1) * m + (route >> 1) * rows + y * cap
        row = jnp.where(kept == 1, base.astype(F32) + slot, -1.0)
        info[y, c.e + k : c.e + k + 1, :] = row
    logit_grad = (probs * (prob_grad - jnp.sum(probs * prob_grad, axis=0, keepdims=True))).astype(BF16)
    info[y, 0 : c.e, :] = logit_grad.astype(F32)

    def info_copy(d):
        return remote(info.at[y], info.at[y], sem_info, (d - 1,), to_y(d))

    for d in (2, 1, 3):
        info_copy(d).start()
    for d in (2, 1, 3):
        tok_copy(1, d).start()
    for h in range(2):
        tok[h, y] = tok_send[h, y]
    w_step(0, 2, 1)
    for s in range(3, half):
        for piece in range(2):
            w_step(0, s, piece)
    for d in range(1, NY):
        ref = info.at[at_y(-d)]
        remote(ref, ref, sem_info, (d - 1,), to_y(-d)).wait_recv()

    def wait_tok(h):
        for d in range(1, NY):
            ref = tok.at[h, at_y(-d)]
            remote(ref, ref, sem_tok, (h, d - 1), to_y(-d)).wait_recv()

    def slot_copy(i, h, d):
        return remote(slots_out.at[i, h, at_x(d)], slots.at[i, h, me], sem_slot, (i, h, d - 1), to_x(d))

    def make_slots(i, h):
        targets = [
            jnp.concatenate([info[j, c.e + k : c.e + k + 1, :] for j in range(NY)], axis=1)
            for k in range(2)
        ]
        tokens = tok[h].reshape(NY * t, hq)

        def slot_rows(owner):
            if h == 0:
                row = lax.broadcasted_iota(jnp.int32, (rows, NY * t), 0) + (i * m + owner * rows)
                row = row.astype(F32)
                hit = (row == targets[0]) | (row == targets[1])
                place[i, owner] = jnp.where(hit, 1.0, 0.0).astype(BF16)
            return nn(place[i, owner], tokens).astype(BF16)

        def step(d, carry):
            slots_out[i, h, at_x(d)] = slot_rows(at_x(d))
            slot_copy(i, h, d).start()
            return carry

        lax.fori_loop(1, nx, step, 0)
        slots[i, h, me] = slot_rows(me)

    wait_tok(0)
    make_slots(0, 0)
    for piece in range(2):
        w_step(0, half, piece)
    for piece in range(2):
        w_step(1, 1, piece)
    wait_tok(1)
    make_slots(0, 1)
    w_step(1, 2, 0)
    make_slots(1, 0)
    w_step(1, 2, 1)
    make_slots(1, 1)
    for s in range(3, half):
        for piece in range(2):
            w_step(1, s, piece)

    lg_all = jnp.concatenate([info[j, 0 : c.e, :] for j in range(NY)], axis=1).astype(BF16)
    for h in range(2):
        span = slice(h * hq, (h + 1) * hq)
        ar0[0 : c.e, span] = nn(lg_all, tok[h].reshape(NY * t, hq))
        total = jnp.zeros((8, hq), F32)
        for j in range(NY):
            back = tn(info[j, 0 : c.e, :].astype(BF16), rw_slices[y, :, span]) * tok[h, j].astype(F32)
            total = total + jnp.sum(back.reshape(t // 8, 8, hq), axis=0)
        gain_acc[:, span] = total
    for copy in late:
        copy.wait()

    def rs_copy(i, way, s):
        sign = 1 if way == 0 else -1
        if s == 0:
            src = part_perm.at[i, at_y(2), pl.ds(way * hb, hb)]
            dst = rs_a.at[i, way]
        else:
            src = part_perm.at[i, at_y(sign + NY)]
            dst = rs_b.at[i, way]
        return remote(src, dst, sem_rs, (i, way, s), to_y(sign + NY))

    def permuted(i, j):
        return nn(order[pl.ds(pl.multiple_of(j * blk, 16), blk), :], part[i])

    def preact_part(i):
        for way in range(2):
            w_recv(i, way, half, way)

        def wait_slots(d, carry):
            for h in range(2):
                ref = slots.at[i, h, at_x(nx - d)]
                remote(ref, ref, sem_slot, (i, h, d - 1), to_x(nx - d)).wait_recv()
            return carry

        lax.fori_loop(1, nx, wait_slots, 0)

        def step(h, carry):
            total = jnp.zeros((2 * rows, c.ff), F32)
            for side in range(2):
                some = slots[i, side, pl.ds(2 * h, 2)].reshape(2 * rows, hq)
                total = total + nn(some, wfull[i, side * hz : (side + 1) * hz].reshape(hq, c.ff))
            part[i, pl.ds(pl.multiple_of(h * 2 * rows, 16), 2 * rows), :] = total.astype(BF16)
            return carry

        lax.fori_loop(0, nx // 2, step, 0)
        part_perm[i, at_y(2)] = permuted(i, at_y(2)).astype(BF16)
        for way in range(2):
            rs_copy(i, way, 0).start()

    def preact_relay(i):
        for way, sign in ((0, 1), (1, -1)):
            j = at_y(sign + NY)
            mine = permuted(i, j)
            ref = rs_a.at[i, way]
            remote(ref, ref, sem_rs, (i, way, 0), to_y(NY - sign)).wait_recv()
            span = slice(way * hb, (way + 1) * hb)
            other = slice((1 - way) * hb, (2 - way) * hb)
            part_perm[i, j, span] = (mine[span] + rs_a[i, way].astype(F32)).astype(BF16)
            part_perm[i, j, other] = mine[other].astype(BF16)
            rs_copy(i, way, 1).start()
        part_perm[i, y] = permuted(i, y).astype(BF16)

    def pg_copy(i, way, s):
        sign = 1 if way == 0 else -1
        if s == 0:
            ref = pre_grad.at[i, y]
        else:
            ref = pre_grad.at[i, at_y(NY - sign), pl.ds(way * hb, hb)]
        return remote(ref, ref, sem_pg, (i, way, s), to_y(sign + NY))

    def pg_recv(i, way, s):
        sign = 1 if way == 0 else -1
        if s == 0:
            ref = pre_grad.at[i, at_y(NY - sign)]
        else:
            ref = pre_grad.at[i, at_y(2), pl.ds(way * hb, hb)]
        remote(ref, ref, sem_pg, (i, way, s), to_y(NY - sign)).wait_recv()

    def make_pre_grad(i):
        for way, sign in ((0, 1), (1, -1)):
            ref = rs_b.at[i, way]
            remote(ref, ref, sem_rs, (i, way, 1), to_y(NY - sign)).wait_recv()
        preact = part_perm[i, y].astype(F32) + rs_b[i, 0].astype(F32) + rs_b[i, 1].astype(F32)
        pre_grad[i, y] = (grad_hidden[i].astype(F32) * silu_slope(preact)).astype(BF16)
        for way in range(2):
            pg_copy(i, way, 0).start()

    def relay_pre_grad(i):
        for way in range(2):
            pg_recv(i, way, 0)
            pg_copy(i, way, 1).start()

    def back_copy(i, h, d):
        return remote(backs.at[i, h, at_x(d)], returned.at[i, h, me], sem_back, (i, h, d - 1), to_x(d))

    def wg_copy(i, way, s):
        sign = 1 if way == 0 else -1
        src, dst = wg_out.at[i, way, s - 1], wg_in.at[i, way, s - 1]
        if s == 1:
            src, dst = src.at[pl.ds(way * hc, hc)], dst.at[pl.ds(way * hc, hc)]
        return remote(src, dst, sem_wg, (i, way, s - 1), to_z(sign))

    def wg_recv(i, way, s):
        sign = 1 if way == 0 else -1
        ref = wg_in.at[i, way, s - 1]
        if s == 1:
            ref = ref.at[pl.ds(way * hc, hc)]
        remote(ref, ref, sem_wg, (i, way, s - 1), to_z(-sign)).wait_recv()

    def weight_grad(i, owner):
        inside = pl.ds(pl.multiple_of((owner % hz) * cb, cb), cb)
        left = slots[i, owner // hz, :, :, inside].reshape(m, cb)
        return tn(left, pg_rows[i])

    def wg_step(i, s):
        if s == 1:
            block = weight_grad(i, at_z(half)).astype(BF16)
            for way in range(2):
                span = slice(way * hc, (way + 1) * hc)
                wg_out[i, way, 0, span] = block[span]
                wg_copy(i, way, 1).start()
            return
        for way, sign in ((0, 1), (1, -1)):
            block = weight_grad(i, at_z(sign * (half + 1 - s)))
            wg_recv(i, way, s - 1)
            if s == 2:
                span = slice(way * hc, (way + 1) * hc)
                other = slice((1 - way) * hc, (2 - way) * hc)
                wg_out[i, way, 1, span] = (block[span] + wg_in[i, way, 0, span].astype(F32)).astype(BF16)
                wg_out[i, way, 1, other] = block[other].astype(BF16)
            else:
                wg_out[i, way, s - 1] = (block + wg_in[i, way, s - 2].astype(F32)).astype(BF16)
            wg_copy(i, way, s).start()

    def back_part(i):
        for way in range(2):
            pg_recv(i, way, 1)
        grads = pre_grad[i].reshape(m, c.ff)

        def unpermute(h, carry):
            span = pl.ds(pl.multiple_of(h * 2 * rows, 16), 2 * rows)
            pg_rows[i, span, :] = nn(order_t[span, :], grads).astype(BF16)
            return carry

        lax.fori_loop(0, nx // 2, unpermute, 0)
        wide = 2 * cb
        for h in range(2):
            for b in range(hq // wide):
                span = slice(b * wide, (b + 1) * wide)
                first = h * hz + 2 * b
                out = nt(pg_rows[i], wfull[i, first : first + 2].reshape(wide, c.ff)).astype(BF16)
                backs[i, h, :, :, span] = out.reshape(nx, rows, wide)
                terms = out.astype(F32) * slots[i, h, :, :, span].reshape(m, wide).astype(F32)
                where = slice(h * hq + b * wide, h * hq + (b + 1) * wide)
                gain_acc[:, where] += jnp.sum(terms.reshape(m // 8, 8, wide), axis=0)
            if i == 0:
                send_backs(i, h)
            if h == 0:
                wg_step(i, 1)

    def send_backs(i, h):
        def step(d, carry):
            back_copy(i, h, d).start()
            return carry

        lax.fori_loop(1, nx, step, 0)
        returned[i, h, me] = backs[i, h, me]

    def combine(i, h):
        def wait_backs(d, carry):
            ref = returned.at[i, h, at_x(nx - d)]
            remote(ref, ref, sem_back, (i, h, d - 1), to_x(nx - d)).wait_recv()
            return carry

        lax.fori_loop(1, nx, wait_backs, 0)
        got = returned[i, h].reshape(m, hq)
        span = slice(h * hq, (h + 1) * hq)
        for j in range(NY):
            there = place[i, :, :, j * t : (j + 1) * t].reshape(m, t)
            if i == 0:
                acc[j, :, span] = tn(there, got)
            else:
                tok_back[h, j] = (acc[j, :, span] + tn(there, got)).astype(BF16)

    def ret_copy(h, d):
        return remote(tok_back.at[h, at_y(d)], tok_ret.at[h, y], sem_ret, (h, d - 1), to_y(d))

    def send_ret(h):
        for d in (2, 1, 3):
            ret_copy(h, d).start()
        tok_ret[h, y] = tok_back[h, y]

    def ar0_slice(e):
        return ar0.at[:, pl.ds(pl.multiple_of(e * cb, cb), cb)]

    def ar_x(d):
        return remote(ar0_slice(at_x(d)), ar1.at[me], sem_ar, (0, d - 1), to_x(d))

    def ar_z(d):
        return remote(ar2.at[z], ar2.at[z], sem_ar, (1, d - 1), to_z(d))

    def ar_y(d):
        return remote(ar3.at[y], ar3.at[y], sem_ar, (2, d - 1), to_y(d))

    def ar_out(d):
        return remote(ar3, ar4.at[me], sem_ar, (3, d - 1), to_x(d))

    def wait_ar(index, ref, target):
        remote(ref, ref, sem_ar, index, target).wait_recv()

    preact_part(0)
    for piece in range(2):
        w_step(1, half, piece)
    preact_relay(0)
    make_pre_grad(0)
    preact_part(1)
    relay_pre_grad(0)
    preact_relay(1)
    back_part(0)
    make_pre_grad(1)
    wg_step(0, 2)
    relay_pre_grad(1)
    wg_step(0, 3)
    back_part(1)

    ar0[c.e : c.e + 8, :] = gain_acc[...]
    for d in range(1, nx):
        ar_x(d).start()
    send_backs(1, 0)
    send_backs(1, 1)
    ar1[me] = ar0[:, pl.ds(pl.multiple_of(me * cb, cb), cb)]
    for s in range(4, half + 1):
        wg_step(0, s)
    for h in range(2):
        combine(0, h)
    for d in range(1, nx):
        wait_ar((0, d - 1), ar1.at[at_x(nx - d)], to_x(nx - d))
    ar2[z] = jnp.sum(ar1[...], axis=0)
    for d in range(1, nz):
        ar_z(d).start()
    wg_step(1, 2)
    for d in range(1, nz):
        wait_ar((1, d - 1), ar2.at[at_z(-d)], to_z(-d))
    ar3[y] = jnp.sum(ar2[...], axis=0)
    for d in range(1, NY):
        ar_y(d).start()
    combine(1, 0)
    send_ret(0)
    wg_step(1, 3)
    for d in range(1, NY):
        wait_ar((2, d - 1), ar3.at[at_y(NY - d)], to_y(NY - d))
    ar4[me] = ar3[...]
    for d in range(1, nx):
        ar_out(d).start()
    for i in range(2):
        wg_own[i] = weight_grad(i, z)
    for s in range(4, half + 1):
        wg_step(1, s)
    for way in range(2):
        wg_recv(0, way, half)
    up_out[:, 0, :] = wg_own[0] + wg_in[0, 0, half - 1].astype(F32) + wg_in[0, 1, half - 1].astype(F32)
    combine(1, 1)
    send_ret(1)

    for d in range(1, nx):
        wait_ar((3, d - 1), ar4.at[at_x(nx - d)], to_x(nx - d))
    for e in range(nx):
        for j in range(NY):
            span = slice((e * NY + j) * cb, (e * NY + j + 1) * cb)
            router_out[:, span] = ar4[e, j, 0 : c.e]
            total = jnp.sum(ar4[e, j, c.e : c.e + 8], axis=0, keepdims=True)
            gain_out[:, span] = total / norm_gain[:, span]

    inv = inv_ref[...]
    grads = info[y, 0 : c.e, :].astype(BF16)
    inner = jnp.zeros((t, cb), F32)
    for h in range(2):
        if h == 1:
            for way in range(2):
                wg_recv(1, way, half)
            up_out[:, 1, :] = wg_own[1] + wg_in[1, 0, half - 1].astype(F32) + wg_in[1, 1, half - 1].astype(F32)
        for d in range(1, NY):
            ref = tok_ret.at[h, at_y(NY - d)]
            remote(ref, ref, sem_ret, (h, d - 1), to_y(NY - d)).wait_recv()
        for p in range(NY):
            half_span = slice(h * hq, (h + 1) * hq)
            acc[p, :, half_span] = tn(grads, rw_slices[p, :, half_span]) + tok_ret[h, p].astype(F32)
        for b in range(h * hz * NY, (h + 1) * hz * NY):
            span = slice(b * cb, (b + 1) * cb)
            here = slice((b // NY) * cb, (b // NY + 1) * cb)
            inner = inner + acc[b % NY, :, here] * norm_gain[:, span] * residual[:, span].astype(F32)
    mean = jnp.sum(inner, axis=1, keepdims=True) * (1.0 / c.d)
    scale = inv * inv * inv * mean
    for b in range(nz * NY):
        span = slice(b * cb, (b + 1) * cb)
        here = slice((b // NY) * cb, (b // NY + 1) * cb)
        scaled = acc[b % NY, :, here] * norm_gain[:, span]
        wide = residual[:, span].astype(F32)
        resid_out[:, span] = (inv * scaled - wide * scale).astype(BF16)

    for i in range(2):
        for way in range(2):
            for s in range(1, half + 1):
                for piece in range(2):
                    if s < half or way == piece:
                        w_copy(i, way, s, piece).wait_send()
                wg_copy(i, way, s).wait_send()
            for s in range(2):
                rs_copy(i, way, s).wait_send()
                pg_copy(i, way, s).wait_send()
        for h in range(2):
            for d in range(1, nx):
                slot_copy(i, h, d).wait_send()
                back_copy(i, h, d).wait_send()
    for d in range(1, NY):
        for h in range(2):
            tok_copy(h, d).wait_send()
            ret_copy(h, d).wait_send()
        info_copy(d).wait_send()
        ar_y(d).wait_send()
    for d in range(1, nx):
        ar_x(d).wait_send()
        ar_out(d).wait_send()
    for d in range(1, nz):
        ar_z(d).wait_send()


def group_order(c):
    out = np.arange(c.m)
    group, sender, slot = out // c.blk, out % c.blk // c.cap, out % c.cap
    source = sender * c.rows + group * c.cap + slot
    table = np.zeros((c.m, c.m), np.float32)
    table[out, source] = 1.0
    return table


def local(
    mesh, residual, norm_gain, router_weight, up_weight, routes, keep_flags, gate_grad, grad_hidden
):
    c = Dims(
        mesh,
        residual.shape[0],
        residual.shape[1],
        up_weight.shape[2],
        grad_hidden.shape[1] // mesh.shape["expert"],
    )
    order = group_order(c)
    half = c.nz // 2
    dma = pltpu.SemaphoreType.DMA
    most = max(c.nz, c.nx) - 1
    vmem = pl.BlockSpec(memory_space=pltpu.VMEM)
    hbm = pl.BlockSpec(memory_space=pl.ANY)
    resid_grad, up_grad, router_grad, gain_grad = pl.pallas_call(
        functools.partial(kernel, c),
        out_shape=(
            jax.ShapeDtypeStruct((c.t, c.d), BF16),
            jax.ShapeDtypeStruct((c.cb, 2, c.ff), F32),
            jax.ShapeDtypeStruct((c.e, c.d), F32),
            jax.ShapeDtypeStruct((1, c.d), F32),
        ),
        in_specs=[hbm, vmem, vmem, hbm, vmem, vmem, vmem, hbm, hbm, hbm],
        out_specs=(vmem,) * 4,
        scratch_shapes=[
            pltpu.VMEM((c.t, c.cb), F32),
            pltpu.VMEM((2, NY, c.t, c.q // 2), BF16),
            pltpu.VMEM((2, NY, c.t, c.q // 2), BF16),
            pltpu.VMEM((NY, c.e + 8, c.t), F32),
            pltpu.VMEM((NY, c.e, c.q), BF16),
            pltpu.VMEM((2, c.nx, c.rows, NY * c.t), BF16),
            pltpu.VMEM((2, 2, c.nx, c.rows, c.q // 2), BF16),
            pltpu.VMEM((2, 2, c.nx, c.rows, c.q // 2), BF16),
            pltpu.VMEM((2, c.nz, c.cb, c.ff), BF16),
            pltpu.VMEM((2, c.m, c.ff), BF16),
            pltpu.VMEM((2, NY, c.blk, c.ff), BF16),
            pltpu.VMEM((2, 2, c.blk // 2, c.ff), BF16),
            pltpu.VMEM((2, 2, c.blk, c.ff), BF16),
            pltpu.VMEM((2, NY, c.blk, c.ff), BF16),
            pltpu.VMEM((2, c.m, c.ff), BF16),
            pltpu.VMEM((2, 2, c.nx, c.rows, c.q // 2), BF16),
            pltpu.VMEM((2, 2, c.nx, c.rows, c.q // 2), BF16),
            pltpu.VMEM((2, 2, half, c.cb, c.ff), BF16),
            pltpu.VMEM((2, 2, half, c.cb, c.ff), BF16),
            pltpu.VMEM((NY, c.t, c.q), F32),
            pltpu.VMEM((2, NY, c.t, c.q // 2), BF16),
            pltpu.VMEM((2, NY, c.t, c.q // 2), BF16),
            pltpu.VMEM((8, c.q), F32),
            pltpu.VMEM((c.e + 8, c.q), F32),
            pltpu.VMEM((c.nx, c.e + 8, c.cb), F32),
            pltpu.VMEM((c.nz, c.e + 8, c.cb), F32),
            pltpu.VMEM((NY, c.e + 8, c.cb), F32),
            pltpu.VMEM((c.nx, NY, c.e + 8, c.cb), F32),
            dma((2, 2, NY - 1)),
            dma((2, NY - 1)),
            dma((2, 2, 2, c.nx - 1)),
            dma((2, 2, 2, half, 2)),
            dma((2, 2, 2, 2)),
            dma((2, 2, 2, 2)),
            dma((2, 2, 2, c.nx - 1)),
            dma((2, 2, 2, half)),
            dma((2, 2, NY - 1)),
            dma((2, 4, most)),
            pltpu.VMEM((c.m, c.m), BF16),
            pltpu.VMEM((c.m, c.m), BF16),
            pltpu.VMEM((2, c.blk, c.ff), BF16),
            pltpu.VMEM((c.t, c.d), BF16),
            pltpu.VMEM((2, c.cb, c.ff), F32),
            dma((6,)),
        ],
        compiler_params=pltpu.CompilerParams(
            collective_id=0, has_side_effects=True, vmem_limit_bytes=60 * 2**20
        ),
        cost_estimate=pl.CostEstimate(
            flops=12 * c.m * c.q * c.ff, bytes_accessed=8 * 2**20, transcendentals=2 * c.blk * c.ff
        ),
    )(
        residual,
        norm_gain.reshape(1, c.d),
        router_weight,
        up_weight.transpose(1, 0, 2),
        routes.T,
        keep_flags.T,
        gate_grad.T,
        grad_hidden,
        jnp.asarray(order, BF16),
        jnp.asarray(order.T, BF16),
    )
    return (resid_grad, up_grad, router_grad, gain_grad.reshape(c.d))


def solution(mesh):
    in_specs = (
        P(("dp", "expert"), None),
        P(),
        P(),
        P("dp", "expert", None),
        P(("dp", "expert"), None),
        P(("dp", "expert"), None),
        P(("dp", "expert"), None),
        P("expert", "dp", None),
    )
    out_specs = (P(("dp", "expert"), None), P("dp", "expert", None), P(), P())
    return jax.shard_map(
        functools.partial(local, mesh), mesh=mesh, in_specs=in_specs, out_specs=out_specs, check_vma=False
    )
```

```python
import functools

import jax
import jax.numpy as jnp
import numpy as np
from jax import lax
from jax.experimental import pallas as pl
from jax.experimental.pallas import tpu as pltpu
from jax.sharding import PartitionSpec as P

NY = 4
BF16 = jnp.bfloat16
F32 = jnp.float32


def nn(a, b):
    return lax.dot_general(a, b, (((1,), (0,)), ((), ())), preferred_element_type=F32)


def nt(a, b):
    return lax.dot_general(a, b, (((1,), (1,)), ((), ())), preferred_element_type=F32)


def tn(a, b):
    return lax.dot_general(a, b, (((0,), (0,)), ((), ())), preferred_element_type=F32)


def silu_slope(v):
    s = jax.nn.sigmoid(v)
    return s * (1.0 + v * (1.0 - s))


class Dims:
    def __init__(self, mesh, tokens, width, ff, cap):
        self.nz = mesh.shape["dp"] // NY
        self.nx = mesh.shape["expert"]
        self.t = tokens
        self.d = width
        self.cb = width // (self.nz * NY)
        self.q = width // NY
        self.ff = ff
        self.cap = cap
        self.e = 2 * self.nx
        self.rows = NY * cap
        self.m = self.nx * self.rows
        self.blk = self.nx * cap


def kernel(
    c,
    residual_hbm,
    norm_gain,
    router_weight,
    weight_hbm,
    routes,
    keep,
    gate,
    grad_hidden_hbm,
    order_hbm,
    order_t_hbm,
    resid_out,
    up_out,
    router_out,
    gain_out,
    inv_ref,
    tok_send,
    tok,
    info,
    rw_slices,
    place,
    slots_out,
    slots,
    wfull,
    part,
    part_perm,
    rs_a,
    rs_b,
    pre_grad,
    pg_rows,
    backs,
    returned,
    wg_out,
    wg_in,
    acc,
    tok_back,
    tok_ret,
    gain_acc,
    ar0,
    ar1,
    ar2,
    ar3,
    ar4,
    sem_tok,
    sem_info,
    sem_slot,
    sem_w,
    sem_rs,
    sem_pg,
    sem_back,
    sem_wg,
    sem_ret,
    sem_ar,
    order,
    order_t,
    grad_hidden,
    residual,
    wg_own,
    weight,
    sem_local,
):
    nz, nx, t, q, cb, cap, rows, m, blk = c.nz, c.nx, c.t, c.q, c.cb, c.cap, c.rows, c.m, c.blk
    half = nz // 2
    hq = q // 2
    hz = nz // 2
    hb = blk // 2
    hc = cb // 2
    dp = lax.axis_index("dp")
    me = lax.axis_index("expert")
    z, y = dp // NY, dp % NY

    def at_y(d):
        return (y + d) % NY

    def at_z(d):
        return (z + d + nz) % nz

    def at_x(d):
        return (me + d) % nx

    def to_y(d):
        return {"dp": z * NY + at_y(d)}

    def to_z(d):
        return {"dp": at_z(d) * NY + y}

    def to_x(d):
        return {"expert": at_x(d)}

    def remote(src, dst, sems, index, target):
        return pltpu.make_async_remote_copy(
            src_ref=src,
            dst_ref=dst,
            send_sem=sems.at[(0, *index)],
            recv_sem=sems.at[(1, *index)],
            device_id=target,
            device_id_type=pl.DeviceIdType.MESH,
        )

    early = [
        pltpu.make_async_copy(residual_hbm, residual, sem_local.at[4]),
        pltpu.make_async_copy(weight_hbm, weight, sem_local.at[3]),
    ]
    for copy in early:
        copy.start()
    late = [
        pltpu.make_async_copy(order_hbm, order, sem_local.at[0]),
        pltpu.make_async_copy(order_t_hbm, order_t, sem_local.at[1]),
        pltpu.make_async_copy(grad_hidden_hbm, grad_hidden, sem_local.at[2]),
    ]
    barrier = pltpu.get_barrier_semaphore()
    for d in range(1, NY):
        pl.semaphore_signal(barrier, inc=1, device_id=to_y(d))
    for d in range(1, nz):
        pl.semaphore_signal(barrier, inc=1, device_id=to_z(d))
    for d in range(1, nx):
        pl.semaphore_signal(barrier, inc=1, device_id=to_x(d))
    pl.semaphore_wait(barrier, NY + nz + nx - 3)

    def w_piece(i, way, s, piece, source):
        sign = 1 if way == 0 else -1
        ref = wfull.at[i, source, pl.ds(piece * hc, hc)]
        return remote(ref, ref, sem_w, (i, way, s - 1, piece), to_z(sign))

    def w_copy(i, way, s, piece):
        sign = 1 if way == 0 else -1
        return w_piece(i, way, s, piece, at_z(-sign * (s - 1)))

    def w_recv(i, way, s, piece):
        sign = 1 if way == 0 else -1
        w_piece(i, way, s, piece, at_z(-sign * s)).wait_recv()

    def w_step(i, s, piece):
        for way in range(2):
            if s > 1:
                w_recv(i, way, s - 1, piece)
            if s < half or way == piece:
                w_copy(i, way, s, piece).start()

    early[0].wait()

    sums = jnp.zeros((t, cb), F32)
    for b in range(nz * NY):
        x = residual[:, b * cb : (b + 1) * cb].astype(F32)
        sums = sums + x * x
    inv_rms = lax.rsqrt(jnp.sum(sums, axis=1, keepdims=True) * (1.0 / c.d) + 1e-06)
    inv_ref[...] = jnp.broadcast_to(inv_rms, inv_ref.shape)

    def norm_slice(h, p):
        for b in range(hz):
            span = pl.ds(pl.multiple_of(((h * hz + b) * NY + p) * cb, cb), cb)
            x = residual[:, span].astype(F32)
            tok_send[h, p, :, b * cb : (b + 1) * cb] = (x * inv_rms * norm_gain[:, span]).astype(BF16)

    def tok_copy(h, d):
        return remote(tok_send.at[h, at_y(d)], tok.at[h, y], sem_tok, (h, d - 1), to_y(d))

    for d in (2, 1, 3):
        norm_slice(0, at_y(d))
        tok_copy(0, d).start()
    early[1].wait()
    for i in range(2):
        wfull[i, z] = weight[:, i, :]
        if i == 0:
            w_step(0, 1, 0)
            w_step(0, 1, 1)
    for copy in late:
        copy.start()
    norm_slice(0, y)
    for p in range(NY):
        norm_slice(1, p)
    w_step(0, 2, 0)
    for b in range(nz * NY):
        inner = slice((b // NY) * cb, (b // NY + 1) * cb)
        rw_slices[b % NY, :, inner] = router_weight[:, b * cb : (b + 1) * cb]

    logits = jnp.zeros((c.e, t), F32)
    for p in range(NY):
        for h in range(2):
            logits = logits + nt(rw_slices[p, :, h * hq : (h + 1) * hq], tok_send[h, p])
    top = jnp.max(logits, axis=0, keepdims=True)
    expo = jnp.exp(logits - top)
    probs = expo / jnp.sum(expo, axis=0, keepdims=True)
    expert_ids = lax.broadcasted_iota(jnp.int32, (c.e, t), 0)
    members = [(expert_ids == routes[k : k + 1, :]) for k in range(2)]
    counts = sum(jnp.where(mk, 1.0, 0.0) for mk in members)
    before = lax.broadcasted_iota(jnp.int32, (t, t), 0) < lax.broadcasted_iota(jnp.int32, (t, t), 1)
    ahead = nn(counts.astype(BF16), jnp.where(before, 1.0, 0.0).astype(BF16))
    prob_grad = jnp.zeros((c.e, t), F32)
    info[y] = jnp.zeros_like(info[y])
    for k in range(2):
        kept = keep[k : k + 1, :]
        prob_grad = prob_grad + jnp.where(members[k], kept.astype(F32) * gate[k : k + 1, :], 0.0)
        slot = jnp.sum(jnp.where(members[k], ahead, 0.0), axis=0, keepdims=True)
        route = routes[k : k + 1, :]
        base = (route & 1) * m + (route >> 1) * rows + y * cap
        row = jnp.where(kept == 1, base.astype(F32) + slot, -1.0)
        info[y, c.e + k : c.e + k + 1, :] = row
    logit_grad = (probs * (prob_grad - jnp.sum(probs * prob_grad, axis=0, keepdims=True))).astype(BF16)
    info[y, 0 : c.e, :] = logit_grad.astype(F32)

    def info_copy(d):
        return remote(info.at[y], info.at[y], sem_info, (d - 1,), to_y(d))

    for d in (2, 1, 3):
        info_copy(d).start()
    for d in (2, 1, 3):
        tok_copy(1, d).start()
    for h in range(2):
        tok[h, y] = tok_send[h, y]
    w_step(0, 2, 1)
    for s in range(3, half):
        for piece in range(2):
            w_step(0, s, piece)
    for d in range(1, NY):
        ref = info.at[at_y(-d)]
        remote(ref, ref, sem_info, (d - 1,), to_y(-d)).wait_recv()

    def wait_tok(h):
        for d in range(1, NY):
            ref = tok.at[h, at_y(-d)]
            remote(ref, ref, sem_tok, (h, d - 1), to_y(-d)).wait_recv()

    def slot_copy(i, h, d):
        return remote(slots_out.at[i, h, at_x(d)], slots.at[i, h, me], sem_slot, (i, h, d - 1), to_x(d))

    def make_slots(i, h):
        targets = [
            jnp.concatenate([info[j, c.e + k : c.e + k + 1, :] for j in range(NY)], axis=1)
            for k in range(2)
        ]
        tokens = tok[h].reshape(NY * t, hq)

        def slot_rows(owner):
            if h == 0:
                row = lax.broadcasted_iota(jnp.int32, (rows, NY * t), 0) + (i * m + owner * rows)
                row = row.astype(F32)
                hit = (row == targets[0]) | (row == targets[1])
                place[i, owner] = jnp.where(hit, 1.0, 0.0).astype(BF16)
            return nn(place[i, owner], tokens).astype(BF16)

        def step(d, carry):
            slots_out[i, h, at_x(d)] = slot_rows(at_x(d))
            slot_copy(i, h, d).start()
            return carry

        lax.fori_loop(1, nx, step, 0)
        slots[i, h, me] = slot_rows(me)

    wait_tok(0)
    make_slots(0, 0)
    for piece in range(2):
        w_step(0, half, piece)
    for piece in range(2):
        w_step(1, 1, piece)
    wait_tok(1)
    make_slots(0, 1)
    w_step(1, 2, 0)
    make_slots(1, 0)
    w_step(1, 2, 1)
    make_slots(1, 1)
    for s in range(3, half):
        for piece in range(2):
            w_step(1, s, piece)

    lg_all = jnp.concatenate([info[j, 0 : c.e, :] for j in range(NY)], axis=1).astype(BF16)
    for h in range(2):
        span = slice(h * hq, (h + 1) * hq)
        ar0[0 : c.e, span] = nn(lg_all, tok[h].reshape(NY * t, hq))
        total = jnp.zeros((8, hq), F32)
        for j in range(NY):
            back = tn(info[j, 0 : c.e, :].astype(BF16), rw_slices[y, :, span]) * tok[h, j].astype(F32)
            total = total + jnp.sum(back.reshape(t // 8, 8, hq), axis=0)
        gain_acc[:, span] = total
    for copy in late:
        copy.wait()

    def rs_copy(i, way, s):
        sign = 1 if way == 0 else -1
        if s == 0:
            src = part_perm.at[i, at_y(2), pl.ds(way * hb, hb)]
            dst = rs_a.at[i, way]
        else:
            src = part_perm.at[i, at_y(sign + NY)]
            dst = rs_b.at[i, way]
        return remote(src, dst, sem_rs, (i, way, s), to_y(sign + NY))

    def permuted(i, j):
        return nn(order[pl.ds(pl.multiple_of(j * blk, 16), blk), :], part[i])

    def preact_part(i):
        for way in range(2):
            w_recv(i, way, half, way)

        chips = nx // 2
        for back in [k for k in range(1, chips) if k < chips - 1] + [0, chips - 1]:
            chip = (me // 2 - back + chips) % chips
            for core in range(2) if back else range(1):
                sender = chip * 2 + (core if back else 1 - me % 2)
                gap = (me - sender + nx) % nx
                for side in range(2):
                    ref = slots.at[i, side, sender]
                    remote(ref, ref, sem_slot, (i, side, gap - 1), {"expert": sender}).wait_recv()
            total = jnp.zeros((2 * rows, c.ff), F32)
            for side in range(2):
                some = slots[i, side, pl.ds(2 * chip, 2)].reshape(2 * rows, hq)
                total = total + nn(some, wfull[i, side * hz : (side + 1) * hz].reshape(hq, c.ff))
            part[i, pl.ds(pl.multiple_of(chip * 2 * rows, 16), 2 * rows), :] = total.astype(BF16)
        part_perm[i, at_y(2)] = permuted(i, at_y(2)).astype(BF16)
        for way in range(2):
            rs_copy(i, way, 0).start()

    def preact_relay(i):
        for way, sign in ((0, 1), (1, -1)):
            j = at_y(sign + NY)
            mine = permuted(i, j)
            ref = rs_a.at[i, way]
            remote(ref, ref, sem_rs, (i, way, 0), to_y(NY - sign)).wait_recv()
            span = slice(way * hb, (way + 1) * hb)
            other = slice((1 - way) * hb, (2 - way) * hb)
            part_perm[i, j, span] = (mine[span] + rs_a[i, way].astype(F32)).astype(BF16)
            part_perm[i, j, other] = mine[other].astype(BF16)
            rs_copy(i, way, 1).start()
        part_perm[i, y] = permuted(i, y).astype(BF16)

    def pg_copy(i, way, s):
        sign = 1 if way == 0 else -1
        if s == 0:
            ref = pre_grad.at[i, y]
        else:
            ref = pre_grad.at[i, at_y(NY - sign), pl.ds(way * hb, hb)]
        return remote(ref, ref, sem_pg, (i, way, s), to_y(sign + NY))

    def pg_recv(i, way, s):
        sign = 1 if way == 0 else -1
        if s == 0:
            ref = pre_grad.at[i, at_y(NY - sign)]
        else:
            ref = pre_grad.at[i, at_y(2), pl.ds(way * hb, hb)]
        remote(ref, ref, sem_pg, (i, way, s), to_y(NY - sign)).wait_recv()

    def make_pre_grad(i):
        for way, sign in ((0, 1), (1, -1)):
            ref = rs_b.at[i, way]
            remote(ref, ref, sem_rs, (i, way, 1), to_y(NY - sign)).wait_recv()
        preact = part_perm[i, y].astype(F32) + rs_b[i, 0].astype(F32) + rs_b[i, 1].astype(F32)
        pre_grad[i, y] = (grad_hidden[i].astype(F32) * silu_slope(preact)).astype(BF16)
        for way in range(2):
            pg_copy(i, way, 0).start()

    def relay_pre_grad(i):
        for way in range(2):
            pg_recv(i, way, 0)
            pg_copy(i, way, 1).start()

    def back_copy(i, h, d):
        return remote(backs.at[i, h, at_x(d)], returned.at[i, h, me], sem_back, (i, h, d - 1), to_x(d))

    def wg_copy(i, way, s):
        sign = 1 if way == 0 else -1
        src, dst = wg_out.at[i, way, s - 1], wg_in.at[i, way, s - 1]
        if s == 1:
            src, dst = src.at[pl.ds(way * hc, hc)], dst.at[pl.ds(way * hc, hc)]
        return remote(src, dst, sem_wg, (i, way, s - 1), to_z(sign))

    def wg_recv(i, way, s):
        sign = 1 if way == 0 else -1
        ref = wg_in.at[i, way, s - 1]
        if s == 1:
            ref = ref.at[pl.ds(way * hc, hc)]
        remote(ref, ref, sem_wg, (i, way, s - 1), to_z(-sign)).wait_recv()

    def weight_grad(i, owner):
        inside = pl.ds(pl.multiple_of((owner % hz) * cb, cb), cb)
        left = slots[i, owner // hz, :, :, inside].reshape(m, cb)
        return tn(left, pg_rows[i])

    def wg_step(i, s):
        if s == 1:
            block = weight_grad(i, at_z(half)).astype(BF16)
            for way in range(2):
                span = slice(way * hc, (way + 1) * hc)
                wg_out[i, way, 0, span] = block[span]
                wg_copy(i, way, 1).start()
            return
        for way, sign in ((0, 1), (1, -1)):
            block = weight_grad(i, at_z(sign * (half + 1 - s)))
            wg_recv(i, way, s - 1)
            if s == 2:
                span = slice(way * hc, (way + 1) * hc)
                other = slice((1 - way) * hc, (2 - way) * hc)
                wg_out[i, way, 1, span] = (block[span] + wg_in[i, way, 0, span].astype(F32)).astype(BF16)
                wg_out[i, way, 1, other] = block[other].astype(BF16)
            else:
                wg_out[i, way, s - 1] = (block + wg_in[i, way, s - 2].astype(F32)).astype(BF16)
            wg_copy(i, way, s).start()

    def back_part(i):
        for way in range(2):
            pg_recv(i, way, 1)
        grads = pre_grad[i].reshape(m, c.ff)

        def unpermute(h, carry):
            span = pl.ds(pl.multiple_of(h * 2 * rows, 16), 2 * rows)
            pg_rows[i, span, :] = nn(order_t[span, :], grads).astype(BF16)
            return carry

        lax.fori_loop(0, nx // 2, unpermute, 0)
        wide = 2 * cb
        for h in range(2):
            for b in range(hq // wide):
                span = slice(b * wide, (b + 1) * wide)
                first = h * hz + 2 * b
                out = nt(pg_rows[i], wfull[i, first : first + 2].reshape(wide, c.ff)).astype(BF16)
                backs[i, h, :, :, span] = out.reshape(nx, rows, wide)
                terms = out.astype(F32) * slots[i, h, :, :, span].reshape(m, wide).astype(F32)
                where = slice(h * hq + b * wide, h * hq + (b + 1) * wide)
                gain_acc[:, where] += jnp.sum(terms.reshape(m // 8, 8, wide), axis=0)
            if i == 0 or h == 0:
                send_backs(i, h)
            if h == 0:
                wg_step(i, 1)

    def send_backs(i, h):
        def step(d, carry):
            back_copy(i, h, d).start()
            return carry

        lax.fori_loop(1, nx, step, 0)
        returned[i, h, me] = backs[i, h, me]

    def combine(i, h):
        def wait_backs(d, carry):
            ref = returned.at[i, h, at_x(nx - d)]
            remote(ref, ref, sem_back, (i, h, d - 1), to_x(nx - d)).wait_recv()
            return carry

        lax.fori_loop(1, nx, wait_backs, 0)
        got = returned[i, h].reshape(m, hq)
        span = slice(h * hq, (h + 1) * hq)
        for d in (2, 1, 3, 0):
            j = at_y(d)
            there = place[i, :, :, pl.ds(pl.multiple_of(j * t, t), t)].reshape(m, t)
            if i == 0:
                acc[j, :, span] = tn(there, got)
            else:
                total = (acc[j, :, span] + tn(there, got)).astype(BF16)
                if d == 0:
                    tok_ret[h, j] = total
                else:
                    tok_back[h, j] = total
                    ret_copy(h, d).start()

    def ret_copy(h, d):
        return remote(tok_back.at[h, at_y(d)], tok_ret.at[h, y], sem_ret, (h, d - 1), to_y(d))

    def ar0_slice(e):
        return ar0.at[:, pl.ds(pl.multiple_of(e * cb, cb), cb)]

    def ar_x(d):
        return remote(ar0_slice(at_x(d)), ar1.at[me], sem_ar, (0, d - 1), to_x(d))

    def ar_z(d):
        return remote(ar2.at[z], ar2.at[z], sem_ar, (1, d - 1), to_z(d))

    def ar_y(d):
        return remote(ar3.at[y], ar3.at[y], sem_ar, (2, d - 1), to_y(d))

    def ar_out(d):
        return remote(ar3, ar4.at[me], sem_ar, (3, d - 1), to_x(d))

    def wait_ar(index, ref, target):
        remote(ref, ref, sem_ar, index, target).wait_recv()

    preact_part(0)
    for piece in range(2):
        w_step(1, half, piece)
    preact_relay(0)
    make_pre_grad(0)
    preact_part(1)
    relay_pre_grad(0)
    preact_relay(1)
    back_part(0)
    make_pre_grad(1)
    wg_step(0, 2)
    relay_pre_grad(1)
    wg_step(0, 3)
    back_part(1)

    ar0[c.e : c.e + 8, :] = gain_acc[...]
    for d in range(1, nx):
        ar_x(d).start()
    send_backs(1, 1)
    ar1[me] = ar0[:, pl.ds(pl.multiple_of(me * cb, cb), cb)]
    for s in range(4, half + 1):
        wg_step(0, s)
    for h in range(2):
        combine(0, h)
    wg_step(1, 2)
    combine(1, 0)
    for d in range(1, nx):
        wait_ar((0, d - 1), ar1.at[at_x(nx - d)], to_x(nx - d))
    ar2[z] = jnp.sum(ar1[...], axis=0)
    for d in range(1, nz):
        ar_z(d).start()
    wg_step(1, 3)
    for d in range(1, nz):
        wait_ar((1, d - 1), ar2.at[at_z(-d)], to_z(-d))
    ar3[y] = jnp.sum(ar2[...], axis=0)
    for d in range(1, NY):
        ar_y(d).start()
    for i in range(2):
        wg_own[i] = weight_grad(i, z)
    for d in range(1, NY):
        wait_ar((2, d - 1), ar3.at[at_y(NY - d)], to_y(NY - d))
    ar4[me] = ar3[...]
    for d in range(1, nx):
        ar_out(d).start()
    for s in range(4, half + 1):
        wg_step(1, s)
    for way in range(2):
        wg_recv(0, way, half)
    up_out[:, 0, :] = wg_own[0] + wg_in[0, 0, half - 1].astype(F32) + wg_in[0, 1, half - 1].astype(F32)
    combine(1, 1)

    for d in range(1, nx):
        wait_ar((3, d - 1), ar4.at[at_x(nx - d)], to_x(nx - d))
    for e in range(nx):
        for j in range(NY):
            span = slice((e * NY + j) * cb, (e * NY + j + 1) * cb)
            router_out[:, span] = ar4[e, j, 0 : c.e]
            total = jnp.sum(ar4[e, j, c.e : c.e + 8], axis=0, keepdims=True)
            gain_out[:, span] = total / norm_gain[:, span]

    inv = inv_ref[...]
    grads = info[y, 0 : c.e, :].astype(BF16)
    inner = jnp.zeros((t, cb), F32)
    for h in range(2):
        if h == 1:
            for way in range(2):
                wg_recv(1, way, half)
            up_out[:, 1, :] = wg_own[1] + wg_in[1, 0, half - 1].astype(F32) + wg_in[1, 1, half - 1].astype(F32)
        for d in range(1, NY):
            ref = tok_ret.at[h, at_y(NY - d)]
            remote(ref, ref, sem_ret, (h, d - 1), to_y(NY - d)).wait_recv()
        for p in range(NY):
            half_span = slice(h * hq, (h + 1) * hq)
            acc[p, :, half_span] = tn(grads, rw_slices[p, :, half_span]) + tok_ret[h, p].astype(F32)
        for b in range(h * hz * NY, (h + 1) * hz * NY):
            span = slice(b * cb, (b + 1) * cb)
            here = slice((b // NY) * cb, (b // NY + 1) * cb)
            inner = inner + acc[b % NY, :, here] * norm_gain[:, span] * residual[:, span].astype(F32)
    mean = jnp.sum(inner, axis=1, keepdims=True) * (1.0 / c.d)
    scale = inv * inv * inv * mean
    for b in range(nz * NY):
        span = slice(b * cb, (b + 1) * cb)
        here = slice((b // NY) * cb, (b // NY + 1) * cb)
        scaled = acc[b % NY, :, here] * norm_gain[:, span]
        wide = residual[:, span].astype(F32)
        resid_out[:, span] = (inv * scaled - wide * scale).astype(BF16)

    for i in range(2):
        for way in range(2):
            for s in range(1, half + 1):
                for piece in range(2):
                    if s < half or way == piece:
                        w_copy(i, way, s, piece).wait_send()
                wg_copy(i, way, s).wait_send()
            for s in range(2):
                rs_copy(i, way, s).wait_send()
                pg_copy(i, way, s).wait_send()
        for h in range(2):
            for d in range(1, nx):
                slot_copy(i, h, d).wait_send()
                back_copy(i, h, d).wait_send()
    for d in range(1, NY):
        for h in range(2):
            tok_copy(h, d).wait_send()
            ret_copy(h, d).wait_send()
        info_copy(d).wait_send()
        ar_y(d).wait_send()
    for d in range(1, nx):
        ar_x(d).wait_send()
        ar_out(d).wait_send()
    for d in range(1, nz):
        ar_z(d).wait_send()


def group_order(c):
    out = np.arange(c.m)
    group, sender, slot = out // c.blk, out % c.blk // c.cap, out % c.cap
    source = sender * c.rows + group * c.cap + slot
    table = np.zeros((c.m, c.m), np.float32)
    table[out, source] = 1.0
    return table


def local(
    mesh, residual, norm_gain, router_weight, up_weight, routes, keep_flags, gate_grad, grad_hidden
):
    c = Dims(
        mesh,
        residual.shape[0],
        residual.shape[1],
        up_weight.shape[2],
        grad_hidden.shape[1] // mesh.shape["expert"],
    )
    order = group_order(c)
    half = c.nz // 2
    dma = pltpu.SemaphoreType.DMA
    most = max(c.nz, c.nx) - 1
    vmem = pl.BlockSpec(memory_space=pltpu.VMEM)
    hbm = pl.BlockSpec(memory_space=pl.ANY)
    resid_grad, up_grad, router_grad, gain_grad = pl.pallas_call(
        functools.partial(kernel, c),
        out_shape=(
            jax.ShapeDtypeStruct((c.t, c.d), BF16),
            jax.ShapeDtypeStruct((c.cb, 2, c.ff), F32),
            jax.ShapeDtypeStruct((c.e, c.d), F32),
            jax.ShapeDtypeStruct((1, c.d), F32),
        ),
        in_specs=[hbm, vmem, vmem, hbm, vmem, vmem, vmem, hbm, hbm, hbm],
        out_specs=(vmem,) * 4,
        scratch_shapes=[
            pltpu.VMEM((c.t, c.cb), F32),
            pltpu.VMEM((2, NY, c.t, c.q // 2), BF16),
            pltpu.VMEM((2, NY, c.t, c.q // 2), BF16),
            pltpu.VMEM((NY, c.e + 8, c.t), F32),
            pltpu.VMEM((NY, c.e, c.q), BF16),
            pltpu.VMEM((2, c.nx, c.rows, NY * c.t), BF16),
            pltpu.VMEM((2, 2, c.nx, c.rows, c.q // 2), BF16),
            pltpu.VMEM((2, 2, c.nx, c.rows, c.q // 2), BF16),
            pltpu.VMEM((2, c.nz, c.cb, c.ff), BF16),
            pltpu.VMEM((2, c.m, c.ff), BF16),
            pltpu.VMEM((2, NY, c.blk, c.ff), BF16),
            pltpu.VMEM((2, 2, c.blk // 2, c.ff), BF16),
            pltpu.VMEM((2, 2, c.blk, c.ff), BF16),
            pltpu.VMEM((2, NY, c.blk, c.ff), BF16),
            pltpu.VMEM((2, c.m, c.ff), BF16),
            pltpu.VMEM((2, 2, c.nx, c.rows, c.q // 2), BF16),
            pltpu.VMEM((2, 2, c.nx, c.rows, c.q // 2), BF16),
            pltpu.VMEM((2, 2, half, c.cb, c.ff), BF16),
            pltpu.VMEM((2, 2, half, c.cb, c.ff), BF16),
            pltpu.VMEM((NY, c.t, c.q), F32),
            pltpu.VMEM((2, NY, c.t, c.q // 2), BF16),
            pltpu.VMEM((2, NY, c.t, c.q // 2), BF16),
            pltpu.VMEM((8, c.q), F32),
            pltpu.VMEM((c.e + 8, c.q), F32),
            pltpu.VMEM((c.nx, c.e + 8, c.cb), F32),
            pltpu.VMEM((c.nz, c.e + 8, c.cb), F32),
            pltpu.VMEM((NY, c.e + 8, c.cb), F32),
            pltpu.VMEM((c.nx, NY, c.e + 8, c.cb), F32),
            dma((2, 2, NY - 1)),
            dma((2, NY - 1)),
            dma((2, 2, 2, c.nx - 1)),
            dma((2, 2, 2, half, 2)),
            dma((2, 2, 2, 2)),
            dma((2, 2, 2, 2)),
            dma((2, 2, 2, c.nx - 1)),
            dma((2, 2, 2, half)),
            dma((2, 2, NY - 1)),
            dma((2, 4, most)),
            pltpu.VMEM((c.m, c.m), BF16),
            pltpu.VMEM((c.m, c.m), BF16),
            pltpu.VMEM((2, c.blk, c.ff), BF16),
            pltpu.VMEM((c.t, c.d), BF16),
            pltpu.VMEM((2, c.cb, c.ff), F32),
            pltpu.VMEM((c.cb, 2, c.ff), BF16),
            dma((5,)),
        ],
        compiler_params=pltpu.CompilerParams(
            collective_id=0, has_side_effects=True, vmem_limit_bytes=60 * 2**20
        ),
        cost_estimate=pl.CostEstimate(
            flops=12 * c.m * c.q * c.ff, bytes_accessed=8 * 2**20, transcendentals=2 * c.blk * c.ff
        ),
    )(
        residual,
        norm_gain.reshape(1, c.d),
        router_weight,
        up_weight,
        routes.T,
        keep_flags.T,
        gate_grad.T,
        grad_hidden,
        jnp.asarray(order, BF16),
        jnp.asarray(order.T, BF16),
    )
    return (resid_grad, up_grad, router_grad, gain_grad.reshape(c.d))


def solution(mesh):
    in_specs = (
        P(("dp", "expert"), None),
        P(),
        P(),
        P("dp", "expert", None),
        P(("dp", "expert"), None),
        P(("dp", "expert"), None),
        P(("dp", "expert"), None),
        P("expert", "dp", None),
    )
    out_specs = (P(("dp", "expert"), None), P("dp", "expert", None), P(), P())
    return jax.shard_map(
        functools.partial(local, mesh), mesh=mesh, in_specs=in_specs, out_specs=out_specs, check_vma=False
    )
```
